32 devices in a mesh: rows: 8 (over z, y), tok: 4 (over x, core).
Axes of the slice: x: 2, y: 2, z: 4, core: 2. Of those that a mesh axis runs over, the one named last changes fastest.
Arguments:
- tokens: bfloat16 [2, 8, 512, 512], P(None, 'rows', 'tok'), may hold values from -6 to 6
- segments: int32 [2, 8, 512], P(None, 'rows', 'tok'), may hold values from 0 to 7, never falling along the last dimension, each value on 1 to 385 neighbouring positions
- cotangent: bfloat16 [2, 8, 512, 512], P(None, 'rows', 'tok'), may hold values from -6 to 6
- query_weight: bfloat16 [512, 512], replicated, may hold values from -0.25 to 0.25
- key_weight: bfloat16 [512, 512], replicated, may hold values from -0.25 to 0.25
- value_weight: bfloat16 [512, 512], replicated, may hold values from -0.25 to 0.25
- out_weight: bfloat16 [512, 512], replicated, may hold values from -2 to 2
- attend_gain: float32 [512], replicated, may hold values from 0.1 to 1.9
- attend_bias: float32 [512], replicated, may hold values from -4 to 4
- inner_weight: bfloat16 [512, 2048], replicated, may hold values from -0.25 to 0.25
- inner_bias: float32 [2048], replicated, may hold values from -6 to 6
- outer_weight: bfloat16 [2048, 512], replicated, may hold values from -0.125 to 0.125
- middle_gain: float32 [512], replicated, may hold values from 0.1 to 1.9
- middle_bias: float32 [512], replicated, may hold values from -4 to 4
- adapter_down: bfloat16 [512, 512], replicated, may hold values from -0.25 to 0.25
- adapter_up: bfloat16 [16, 32, 512], replicated, may hold values from -2 to 2
- joining_query: bfloat16 [512, 512], P('rows'), may hold values from -0.25 to 0.25
- joining_key: bfloat16 [512, 512], P('rows'), may hold values from -0.25 to 0.25
- joining_value: bfloat16 [512, 512], P('rows'), may hold values from -0.25 to 0.25
- final_gain: float32 [512], replicated, may hold values from 0.1 to 1.9
- final_bias: float32 [512], replicated, may hold values from -4 to 4
Outputs:
- output: bfloat16 [2, 8, 512, 512], P(None, 'rows', 'tok')
- input_grad: bfloat16 [2, 8, 512, 512], P(None, 'rows', 'tok')
- query_grad: float32 [512, 512], replicated
- key_grad: float32 [512, 512], replicated
- value_grad: float32 [512, 512], replicated
- out_grad: float32 [512, 512], replicated
- attend_gain_grad: float32 [512], replicated
- attend_bias_grad: float32 [512], replicated
- inner_grad: float32 [512, 2048], replicated
- inner_bias_grad: float32 [2048], replicated
- outer_grad: float32 [2048, 512], replicated
- middle_gain_grad: float32 [512], replicated
- middle_bias_grad: float32 [512], replicated
- joining_query_grad: float32 [512, 512], replicated
- joining_key_grad: float32 [512, 512], replicated
- joining_value_grad: float32 [512, 512], replicated
- final_gain_grad: float32 [512], replicated
- final_bias_grad: float32 [512], replicated
The draws below stay inside these ranges and needn't reach their ends.
Inputs may be any that keep to these rules, and one draw needn't show every extreme that they name: `segments`: in every row the segment ids never fall and each document is a run of consecutive tokens; one document of every row has exactly 385 tokens.
All inputs are finite; a program needn't handle non-finite values.
Results may differ from the reference program's by a relative error of at most 0.03.
Values may be sent and summed in bfloat16 or wider, within the bound.
No kernel may reach another device: no remote copies, remote signals or barrier semaphores. Data moves between devices by JAX's collectives and lax.ppermute only.
A program may use at most 128 MiB of HBM per device.

```python
import math
import jax
import jax.numpy as jnp
import numpy as np
from jax import lax

D = 512
FF = 2048
HEAD = 64
NA = 16
R = 32
ROW_LEN = 512
SEGS = 8
ROW_MB = 1
MICRO = 2
ROWS_MB = 8


def levels(own_key, extent, shards, low, largest):
    factor_of, own = 1.0, jax.random.fold_in(own_key, 6)
    for dim, blocks in shards:
        heights = jnp.exp(jax.random.uniform(jax.random.fold_in(own, dim), (blocks,), jnp.float32, low / len(shards), largest / len(shards)))
        factor_of = factor_of * jnp.repeat(heights, extent[dim] // blocks).reshape([-1 if axis == dim else 1 for axis in range(len(extent))])
    return factor_of


def profile(amount, total, limit, skew):
    loads = [(1 << 20) // math.isqrt(standing ** skew) + 1 for standing in range(2, amount + 1)]
    rest, counts = total - limit - (amount - 1), [1] * (amount - 1)
    while rest > 0:
        free = [i for i in range(amount - 1) if counts[i] < limit]
        mass, remaining = sum([loads[i] for i in free]), rest
        for i in free:
            more = min(limit - counts[i], max(1, remaining * loads[i] // mass), rest)
            counts[i] = counts[i] + more
            rest = rest - more
    return np.array([limit] + counts)


def uneven_parts(stream_key, number_of, total, reach, lean):
    if number_of == 2:
        one = jax.random.randint(stream_key, (), max(1, total - reach), min(reach, total - 1) + 1)
        return jnp.stack([one, total - one])
    tallies = jnp.asarray(profile(number_of, total, reach, lean), jnp.int32)
    twos = (number_of - 1) // 2
    donor, sink = tallies[1:1 + 2 * twos:2], tallies[2:2 + 2 * twos:2]
    slack = jnp.minimum(donor - 1, reach - sink)
    shifted = jax.random.randint(jax.random.fold_in(stream_key, 1), (twos,), 0, 1 << 20) % (slack + 1)
    tallies = tallies.at[1:1 + 2 * twos:2].set(donor - shifted).at[2:2 + 2 * twos:2].set(sink + shifted)
    return tallies[jax.random.permutation(jax.random.fold_in(stream_key, 2), number_of)]


def scatter_about(key, dims, spread, most, shards=(), kind=jnp.bfloat16):
    entries = jax.random.normal(key, dims, jnp.float32) * spread
    if len(shards) > 0:
        entries = levels(key, dims, shards, -0.22, 0.18) * entries
    return jnp.clip(entries, min=-most, max=most).astype(kind)


def setup_inputs(seed: int = 0) -> dict:
    arg_keys = jax.random.split(jax.random.key(seed), 22)
    return {
        "tokens": scatter_about(arg_keys[0], (MICRO, ROWS_MB, ROW_LEN, D), 1.0, 6.0, ((1, 8), (2, 4))),
        "segments": jax.vmap(lambda own: jnp.searchsorted(jnp.cumsum(uneven_parts(own, SEGS, ROW_LEN, 3 * ROW_LEN // 4 + 1, 0)), jnp.arange(ROW_LEN), side="right"))(jax.random.split(arg_keys[1], MICRO * ROWS_MB)).reshape((MICRO, ROWS_MB, ROW_LEN)).astype(jnp.int32),
        "cotangent": scatter_about(arg_keys[2], (MICRO, ROWS_MB, ROW_LEN, D), 1.0, 6.0, ((1, 8), (2, 4))),
        "query_weight": scatter_about(arg_keys[3], (D, D), D ** -0.5, 0.25),
        "key_weight": scatter_about(arg_keys[4], (D, D), D ** -0.5, 0.25),
        "value_weight": scatter_about(arg_keys[5], (D, D), D ** -0.5, 0.25),
        "out_weight": scatter_about(arg_keys[6], (D, D), (D * 8 // ROW_LEN) ** -0.5, 2.0),
        "attend_gain": jnp.clip(1.0 + 0.18 * jax.random.normal(arg_keys[7], (D,), jnp.float32), 0.1, 1.9),
        "attend_bias": scatter_about(arg_keys[8], (D,), 0.3, 4.0, (), jnp.float32),
        "inner_weight": scatter_about(arg_keys[9], (D, FF), D ** -0.5, 0.25),
        "inner_bias": scatter_about(arg_keys[10], (FF,), 0.5, 6.0, (), jnp.float32),
        "outer_weight": scatter_about(arg_keys[11], (FF, D), FF ** -0.5, 0.125),
        "middle_gain": jnp.clip(1.0 + 0.18 * jax.random.normal(arg_keys[12], (D,), jnp.float32), 0.1, 1.9),
        "middle_bias": scatter_about(arg_keys[13], (D,), 0.3, 4.0, (), jnp.float32),
        "adapter_down": scatter_about(arg_keys[14], (D, NA * R), D ** -0.5, 0.25),
        "adapter_up": scatter_about(arg_keys[15], (NA, R, D), (R // 4) ** -0.5, 2.0),
        "joining_query": scatter_about(arg_keys[16], (D, D), D ** -0.5, 0.25, ((0, 8),)),
        "joining_key": scatter_about(arg_keys[17], (D, D), D ** -0.5, 0.25, ((0, 8),)),
        "joining_value": scatter_about(arg_keys[18], (D, D), D ** -0.5, 0.25, ((0, 8),)),
        "final_gain": jnp.clip(1.0 + 0.18 * jax.random.normal(arg_keys[19], (D,), jnp.float32), 0.1, 1.9),
        "final_bias": scatter_about(arg_keys[20], (D,), 0.3, 4.0, (), jnp.float32),
    }


@jax.custom_vjp
def low(v):
    return lax.optimization_barrier(v.astype(jnp.bfloat16)).astype(jnp.float32)

@jax.custom_vjp
def low_back(v):
    return v

def low_keep(v):
    return (low(v), None)

def low_pass(kept, grad):
    return (grad,)

def back_keep(v):
    return (v, None)

def back_low(kept, grad):
    return (low(grad),)
low.defvjp(low_keep, low_pass)
low_back.defvjp(back_keep, back_low)
norm_eps = 1e-06

def round_both(operand):
    return low(low_back(operand))

def matmul(left_side, right_side):
    return jnp.dot(left_side, right_side, precision=lax.Precision.HIGHEST)

def normalize(values, norm_gain, norm_shift):
    row_mean = lax.optimization_barrier(jnp.mean(values, -1, keepdims=True))
    centered = values - row_mean
    inv_std = lax.rsqrt(lax.optimization_barrier(jnp.mean(centered * centered, -1, keepdims=True)) + norm_eps)
    return centered * inv_std * norm_gain + norm_shift

def layer_block(params, rows_in, seg_rows):
    query_weight, key_weight, value_weight, out_weight, attend_gain, attend_bias, inner_weight, inner_bias, outer_weight, middle_gain, middle_bias, adapter_down, adapter_up, joining_query, joining_key, joining_value, final_gain, final_bias = params
    row_count, row_length, model_width = rows_in.shape
    head_count = model_width // HEAD
    highest = lax.Precision.HIGHEST
    tok_flat = rows_in.reshape(-1, model_width)
    queries = round_both(matmul(tok_flat, query_weight)).reshape(row_count, row_length, head_count, HEAD)
    key_rows = round_both(matmul(tok_flat, key_weight)).reshape(row_count, row_length, head_count, HEAD)
    value_rows = round_both(matmul(tok_flat, value_weight)).reshape(row_count, row_length, head_count, HEAD)
    scores = jnp.einsum('bqhe,bkhe->bhqk', queries, key_rows, precision=highest) * HEAD ** (-0.5)
    scores = low_back(scores)
    same_doc = (seg_rows[:, :, None] == seg_rows[:, None, :])[:, None]
    scores = jnp.where(same_doc, scores, -1e+30)
    attn_probs = low(jax.nn.softmax(scores, axis=-1))
    attended = round_both(jnp.einsum('bhqk,bkhe->bqhe', attn_probs, value_rows, precision=highest))
    attended = attended.reshape(-1, model_width)
    attn_out = low_back(matmul(attended, out_weight))
    first_norm = normalize(tok_flat + attn_out, attend_gain, attend_bias)
    inner_pre = low_back(matmul(low(first_norm), inner_weight) + inner_bias)
    active = low(jax.nn.gelu(inner_pre, approximate=False))
    outer_out = low_back(matmul(active, outer_weight))
    hidden = normalize(first_norm + outer_out, middle_gain, middle_bias)
    hidden_low = low(hidden)
    down_pre = low_back(matmul(hidden_low, adapter_down))
    bottle_act = low(jax.nn.gelu(down_pre, approximate=False)).reshape(-1, NA, R)
    branch = low_back(jnp.einsum('tnr,nrd->tnd', bottle_act, adapter_up, precision=highest))
    adapted = low(hidden[:, None, :] + branch)
    join_query = round_both(matmul(hidden_low, joining_query))
    join_probe = round_both(matmul(join_query, joining_key.T))
    join_scores = low_back(jnp.einsum('tnd,td->tn', adapted, join_probe, precision=highest) * model_width ** (-0.5))
    join_weights = low(jax.nn.softmax(join_scores, axis=-1))
    join_mixed = round_both(jnp.einsum('tn,tnd->td', join_weights, adapted, precision=highest))
    join_out = low_back(matmul(join_mixed, joining_value))
    final_norm = normalize(hidden + join_out, final_gain, final_bias)
    return final_norm.reshape(row_count, row_length, model_width)

def reference(tokens, segments, cotangent, query_weight, key_weight, value_weight, out_weight, attend_gain, attend_bias, inner_weight, inner_bias, outer_weight, middle_gain, middle_bias, adapter_down, adapter_up, joining_query, joining_key, joining_value, final_gain, final_bias):
    params = tuple((weight.astype(jnp.float32) for weight in (query_weight, key_weight, value_weight, out_weight, attend_gain, attend_bias, inner_weight, inner_bias, outer_weight, middle_gain, middle_bias, adapter_down, adapter_up, joining_query, joining_key, joining_value, final_gain, final_bias)))
    rows_in = tokens.astype(jnp.float32).reshape(-1, ROW_MB, ROW_LEN, D)
    seg_blocks = segments.reshape(-1, ROW_MB, ROW_LEN)

    def forward(rows_all, weights):

        def block_fn(pair):
            return layer_block(weights, pair[0], pair[1])
        return lax.map(jax.checkpoint(block_fn), (rows_all, seg_blocks))
    result, pullback = jax.vjp(forward, rows_in, params)
    grad_in, grad_params = pullback(cotangent.astype(jnp.float32).reshape(result.shape))
    output = result.reshape(tokens.shape).astype(jnp.bfloat16)
    input_grad = grad_in.reshape(tokens.shape).astype(jnp.bfloat16)
    return (output, input_grad, grad_params[0], grad_params[1], grad_params[2], grad_params[3], grad_params[4], grad_params[5], grad_params[6], grad_params[7], grad_params[8], grad_params[9], grad_params[10], grad_params[13], grad_params[14], grad_params[15], grad_params[16], grad_params[17])
```

```python
import functools

import jax
import jax.numpy as jnp
from jax import lax
from jax.experimental import pallas as pl
from jax.experimental.pallas import tpu as pltpu
from jax.sharding import PartitionSpec as P

HEAD = 64
AXES = ("rows", "tok")
BF = jnp.bfloat16
F32 = jnp.float32
norm_eps = 1e-06

ORDER_XY = ((1, 2, 3, 4), (2, 1, 4, 3))
ORDER_Z = ((3, 4, 1, 2), (4, 3, 2, 1))
ORDER_JOIN = ((2, 3, 4), (2, 4, 3))
GROUP = 32
HALF = GROUP // 2

VM = pl.BlockSpec(memory_space=pltpu.VMEM)
ANY = pl.BlockSpec(memory_space=pl.ANY)


def dot(left, right):
    return jnp.dot(left, right, preferred_element_type=F32)


def dot_tn(left, right):
    return lax.dot_general(left, right, (((0,), (0,)), ((), ())), preferred_element_type=F32)


def dot_nt(left, right):
    return lax.dot_general(left, right, (((1,), (1,)), ((), ())), preferred_element_type=F32)


def low(values):
    return values.astype(BF)


def normalize(values, gain, shift):
    centered = values - jnp.mean(values, -1, keepdims=True)
    inv_std = lax.rsqrt(jnp.mean(centered * centered, -1, keepdims=True) + norm_eps)
    unit = centered * inv_std
    return unit * gain + shift, unit, inv_std


def normalize_back(upstream, unit, inv_std, gain):
    grad_unit = upstream * gain
    projected = grad_unit - jnp.mean(grad_unit, -1, keepdims=True)
    projected = projected - unit * jnp.mean(grad_unit * unit, -1, keepdims=True)
    gain_term = jnp.sum(upstream * unit, 0, keepdims=True)
    return projected * inv_std, gain_term, jnp.sum(upstream, 0, keepdims=True)


def gelu_both(values):
    normal_cdf = 0.5 * (1.0 + lax.erf(values * 0.7071067811865476))
    slope = normal_cdf + values * jnp.exp(-0.5 * values * values) * 0.3989422804014327
    return values * normal_cdf, slope


def device_number():
    return lax.axis_index("rows") * 4 + lax.axis_index("tok")


def bit_of(number, bit):
    return lax.rem(lax.div(number, 1 << bit), 2)


def own_place(number, orders, core):
    def along(order):
        total = 0
        for bit in order:
            total = total * 2 + bit_of(number, bit)
        return total

    return jnp.where(core == 0, along(orders[0]), along(orders[1]))


def block_copies(full, keep, send, sems, orders, rows_each):
    me = device_number()
    core = bit_of(me, 0)
    copies = []
    for which, target in ((0, keep), (1, send)):
        half = core if which == 0 else 1 - core
        place = own_place(me, orders, half)
        for spot in range(HALF):
            block = half * HALF + jnp.bitwise_xor(place, spot)
            source = full.at[pl.ds(pl.multiple_of(block * rows_each, rows_each), rows_each), :]
            copies.append(
                pltpu.make_async_copy(
                    source, target.at[pl.ds(spot * rows_each, rows_each), :], sems.at[which, spot]
                )
            )
    return copies


def forward_kernel(
    x0, x1, x2, x3, seg_own, seg_sib, wq, wk, wv, wo, wi, wu, wd, ag, ab, bi, mg, mb,
    qs_ref, k_ref, v_ref, p_ref, o_ref, n1_ref, rs1_ref, al_ref, u_ref, sz_ref,
    n2_ref, rs2_ref, h_ref, c_ref, st_ref, bias,
):
    pieces = (x0, x1, x2, x3)
    tokens_here, width = x0.shape
    batches = seg_own.shape[0] // 2
    length = tokens_here // batches
    qs_ref[...] = low(low(dot(x0[...], wq[...])) * HEAD ** (-0.5))
    for index, piece in enumerate(pieces):
        k_ref[pl.ds(index * tokens_here, tokens_here), :] = low(dot(piece[...], wk[...]))
        v_ref[pl.ds(index * tokens_here, tokens_here), :] = low(dot(piece[...], wv[...]))
    own = seg_own[...].astype(F32)
    sib = seg_sib[...].astype(F32)
    lane = lax.broadcasted_iota(jnp.int32, (1, 2 * HEAD), 1)
    first = (lane < HEAD).astype(BF)
    second = (lane >= HEAD).astype(BF)
    for batch in range(batches):
        query_seg = own[batch : batch + 1, :]
        rows = (
            own[batch : batch + 1, :],
            sib[batch : batch + 1, :],
            own[batches + batch : batches + batch + 1, :],
            sib[batches + batch : batches + batch + 1, :],
        )
        for index, row in enumerate(rows):
            key_seg = jnp.transpose(jnp.broadcast_to(row, (length, length)))
            bias[pl.ds(index * length, length), :] = jnp.where(key_seg == query_seg, 0.0, -1e30)
        both = jnp.concatenate([bias[...], bias[...]], 1)
        for pair in range(width // (2 * HEAD)):
            lanes = slice(pair * 2 * HEAD, (pair + 1) * 2 * HEAD)
            spans = [
                slice(index * tokens_here + batch * length, index * tokens_here + (batch + 1) * length)
                for index in range(4)
            ]
            kp = jnp.concatenate([k_ref[span, lanes] for span in spans], 0)
            vp = jnp.concatenate([v_ref[span, lanes] for span in spans], 0)
            qp = qs_ref[batch * length : (batch + 1) * length, lanes]
            stacked = jnp.concatenate([qp * first, qp * second], 0)
            scores = dot_nt(kp, stacked) + both
            exps = jnp.exp(scores - jnp.max(scores, 0, keepdims=True))
            probs = low(exps * (1.0 / jnp.sum(exps, 0, keepdims=True)))
            p_ref[batch * (width // (2 * HEAD)) + pair] = probs
            mixed = dot_tn(vp, probs)
            joined = jnp.concatenate([mixed[:HEAD, :length], mixed[HEAD:, length:]], 0)
            o_ref[batch * length : (batch + 1) * length, lanes] = low(jnp.transpose(joined))
    residual = x0[...].astype(F32) + dot(o_ref[...], wo[...])
    first_norm, unit, inv_std = normalize(residual, ag[...], ab[...])
    n1_ref[...] = unit
    rs1_ref[...] = jnp.broadcast_to(inv_std, rs1_ref.shape)
    al = low(first_norm)
    al_ref[...] = al
    outer = first_norm
    for part in range(wi.shape[1] // width):
        span = slice(part * width, (part + 1) * width)
        inner = dot(al, wi[:, span]) + bi[:, span]
        active, slope = gelu_both(inner)
        u_ref[:, span] = low(active)
        sz_ref[:, span] = low(slope)
        outer = outer + dot(low(active), wu[span, :])
    hidden, unit, inv_std = normalize(outer, mg[...], mb[...])
    n2_ref[...] = unit
    rs2_ref[...] = jnp.broadcast_to(inv_std, rs2_ref.shape)
    h_ref[...] = hidden
    active, slope = gelu_both(dot(low(hidden), wd[...]))
    c_ref[...] = low(active)
    st_ref[...] = low(slope)


def joining_kernel(
    gathered, bottleneck, adapters, h_ref, c_ref, st_ref, up, cot, fg, fb, *rest
):
    if gathered:
        jw_in, rest = rest[:4], rest[4:]
    else:
        jw_in, rest = rest[:1], rest[1:]
    out_ref, keep, send, dhp_ref, dt_ref, vec_ref, wj, full, sems, jsems = rest
    width = h_ref.shape[1]
    scale = width ** (-0.5)
    me = device_number()
    core = bit_of(me, 0)
    loads = []
    if gathered:
        shard = jw_in[0].shape[2]
        column = jw_in[0].shape[3]
        for which in range(2):
            half = core if which == 0 else 1 - core
            place = own_place(me, tuple(order[::-1] for order in ORDER_JOIN), half)
            for spot in range(8):
                mixed = jnp.bitwise_xor(place, spot)
                swapped = (
                    lax.rem(mixed, 2)
                    + lax.rem(lax.div(mixed, 2), 2) * 4
                    + lax.rem(lax.div(mixed, 4), 2) * 2
                )
                owner = jnp.where(half == 0, mixed, swapped)
                target = wj.at[
                    :,
                    pl.ds(pl.multiple_of(owner * shard, shard), shard),
                    pl.ds(pl.multiple_of(half * column, column), column),
                ]
                source = jw_in[which * 2 + spot // 4].at[spot % 4]
                loads.append(pltpu.make_async_copy(source, target, jsems.at[which, spot]))
    else:
        loads.append(pltpu.make_async_copy(jw_in[0], wj, jsems.at[0, 0]))
    for load in loads:
        load.start()
    hidden = h_ref[...]
    hidden_low = low(hidden)
    cf = c_ref[...].astype(F32)
    row_group = lax.broadcasted_iota(jnp.int32, (width, 128), 0) // bottleneck
    column_of = lax.broadcasted_iota(jnp.int32, (width, 128), 1)
    member = (row_group == column_of).astype(BF)
    valid = lax.broadcasted_iota(jnp.int32, (1, 128), 1) < adapters

    def per_adapter(values):
        high = low(values)
        rest_of = low(values - high.astype(F32))
        return dot(high, member) + dot(rest_of, member)

    for load in loads:
        load.wait()
    fq = low(dot(hidden_low, wj[0]))
    probe = low(dot_nt(fq, wj[1]))
    probe_f = probe.astype(F32)
    up_probe = dot_nt(probe, up[...])
    scores = (
        per_adapter(cf * up_probe) + jnp.sum(hidden * probe_f, -1, keepdims=True)
    ) * scale
    scores = jnp.where(valid, scores, -1e30)
    exps = jnp.exp(scores - jnp.max(scores, -1, keepdims=True))
    weights = exps * (1.0 / jnp.sum(exps, -1, keepdims=True))
    weights_low = low(weights)
    weights_wide = dot_nt(weights_low, member)
    weights_sum = jnp.sum(weights_low.astype(F32), -1, keepdims=True)
    mixed = low(weights_sum * hidden + dot(low(weights_wide * cf), up[...]))
    final, unit, inv_std = normalize(hidden + dot(mixed, wj[2]), fg[...], fb[...])
    out_ref[...] = low(final)
    d3, gain_term, shift_term = normalize_back(cot[...].astype(F32), unit, inv_std, fg[...])
    vec_ref[...] = jnp.concatenate(
        [gain_term, shift_term, jnp.zeros((vec_ref.shape[0] - 2, width), F32)], 0
    )
    dfo = low(d3)
    full[2 * width : 3 * width, :] = low(dot_tn(mixed, dfo))
    dm = low(dot_nt(dfo, wj[2]))
    dm_f = dm.astype(F32)
    up_dm = dot_nt(dm, up[...])
    dw = per_adapter(cf * up_dm) + jnp.sum(hidden * dm_f, -1, keepdims=True)
    df = low(weights * (dw - jnp.sum(weights * dw, -1, keepdims=True)))
    df_wide = dot_nt(df, member)
    df_sum = jnp.sum(df.astype(F32), -1, keepdims=True)
    dr = low((df_sum * hidden + dot(low(df_wide * cf), up[...])) * scale)
    full[width : 2 * width, :] = low(dot_tn(dr, fq))
    dfq = low(dot(dr, wj[1]))
    full[:width, :] = low(dot_tn(hidden_low, dfq))
    copies = block_copies(full, keep, send, sems, ORDER_XY, 3 * width // GROUP)
    for copy in copies:
        copy.start()
    dc = weights_wide * up_dm + (df_wide * scale) * up_probe
    dt_ref[...] = low(dc * st_ref[...].astype(F32))
    dhp_ref[...] = (
        d3 + weights_sum * dm_f + (df_sum * scale) * probe_f + dot_nt(dfq, wj[0])
    )
    for copy in copies:
        copy.wait()


def feed_back_kernel(
    dhp_ref, dt_ref, wd, n2_ref, rs2_ref, mg, u_ref, sz_ref, wi, wu, al_ref, n1_ref, rs1_ref, ag, vec_in,
    d1_ref, vec_ref, keep_u, send_u, keep_i, send_i, full_u, full_i, sems_u, sems_i,
):
    width = dhp_ref.shape[1]
    hidden_grad = dhp_ref[...] + dot_nt(dt_ref[...], wd[...])
    d2, mg_term, mb_term = normalize_back(hidden_grad, n2_ref[...], rs2_ref[:, :1], mg[...])
    dfw = low(d2)
    al = al_ref[...]
    total = d2
    bias_terms = []
    parts = wi.shape[1] // width
    for part in range(parts):
        span = slice(part * width, (part + 1) * width)
        full_u[span, :] = low(dot_tn(u_ref[:, span], dfw))
        dz_wide = dot_nt(dfw, wu[span, :]) * sz_ref[:, span].astype(F32)
        dz = low(dz_wide)
        bias_terms.append(jnp.sum(dz.astype(F32), 0, keepdims=True))
        full_i[span, :] = low(dot_tn(al, dz))
        total = total + dot_nt(dz, wi[:, span])
    copies = block_copies(full_u, keep_u, send_u, sems_u, ORDER_XY, parts * width // GROUP)
    copies += block_copies(full_i, keep_i, send_i, sems_i, ORDER_Z, parts * width // GROUP)
    for copy in copies:
        copy.start()
    d1, ag_term, ab_term = normalize_back(total, n1_ref[...], rs1_ref[:, :1], ag[...])
    d1_ref[...] = d1
    rows = [ag_term, ab_term, mg_term, mb_term, vec_in[0:1, :], vec_in[1:2, :]] + bias_terms
    rows.append(jnp.zeros((vec_ref.shape[0] - len(rows), width), F32))
    vec_ref[...] = jnp.concatenate(rows, 0)
    for copy in copies:
        copy.wait()


def attend_back_kernel(
    d1_ref, wo, o_ref, qs_ref, k_ref, v_ref, p_ref, x0, x1, x2, x3, wq, wk, wv, vec_ref,
    keep, send, gi_own, gi_keep, gi_send, full, dq_scr, dk_scr, dv_scr, do_scr, vec_scr, sems, vsems,
):
    tokens_here, width = x0.shape
    length = p_ref.shape[2] // 2
    batches = tokens_here // length
    pairs = width // (2 * HEAD)
    d1 = d1_ref[...]
    dao = low(d1)
    full[3 * width : 4 * width, :] = low(dot_tn(o_ref[...], dao))
    do_scr[...] = low(dot_nt(dao, wo[...]))
    vec_scr[...] = low(vec_ref[...])
    lane = lax.broadcasted_iota(jnp.int32, (1, 2 * HEAD), 1)
    first = (lane < HEAD).astype(BF)
    second = (lane >= HEAD).astype(BF)
    for batch in range(batches):
        here = slice(batch * length, (batch + 1) * length)
        spans = [
            slice(index * tokens_here + batch * length, index * tokens_here + (batch + 1) * length)
            for index in range(4)
        ]
        for pair in range(pairs):
            lanes = slice(pair * 2 * HEAD, (pair + 1) * 2 * HEAD)
            kp = jnp.concatenate([k_ref[span, lanes] for span in spans], 0)
            vp = jnp.concatenate([v_ref[span, lanes] for span in spans], 0)
            qp = qs_ref[here, lanes]
            dop = do_scr[here, lanes]
            q_stacked = jnp.concatenate([qp * first, qp * second], 0)
            do_stacked = jnp.concatenate([dop * first, dop * second], 0)
            probs = p_ref[batch * pairs + pair]
            weighted = probs.astype(F32) * dot_nt(vp, do_stacked)
            ds = low(weighted - probs.astype(F32) * jnp.sum(weighted, 0, keepdims=True))
            dv = low(dot(probs, do_stacked))
            dk = low(dot(ds, q_stacked))
            for index, span in enumerate(spans):
                rows = slice(index * length, (index + 1) * length)
                dk_scr[span, lanes] = dk[rows, :]
                dv_scr[span, lanes] = dv[rows, :]
            mixed = dot_tn(kp, ds)
            joined = jnp.concatenate([mixed[:HEAD, :length], mixed[HEAD:, length:]], 0)
            dq_scr[here, lanes] = low(jnp.transpose(joined) * HEAD ** (-0.5))
    row_x = jnp.concatenate([x0[...], x1[...], x2[...], x3[...]], 0)
    full[:width, :] = low(dot_tn(x0[...], dq_scr[...]))
    full[width : 2 * width, :] = low(dot_tn(row_x, dk_scr[...]))
    full[2 * width : 3 * width, :] = low(dot_tn(row_x, dv_scr[...]))
    rows_each = 4 * width // GROUP
    copies = block_copies(full, keep, send, sems, ORDER_XY, rows_each)
    for index, target in enumerate((keep, send)):
        spot = target.at[pl.ds(HALF * rows_each, vec_scr.shape[0]), :]
        copies.append(pltpu.make_async_copy(vec_scr, spot, vsems.at[index]))
    for copy in copies:
        copy.start()
    parts = []
    for index in range(4):
        span = slice(index * tokens_here, (index + 1) * tokens_here)
        parts.append(dot_nt(dk_scr[span, :], wk[...]) + dot_nt(dv_scr[span, :], wv[...]))
    gi_own[...] = parts[0] + d1 + dot_nt(dq_scr[...], wq[...])
    gi_keep[...] = low(parts[2])
    gi_send[:tokens_here, :] = low(parts[1])
    gi_send[tokens_here:, :] = low(parts[3])
    for copy in copies:
        copy.wait()


def finish_kernel(orders, columns, with_vec, a8, r1, s8, sr1, *rest):
    if with_vec:
        vec, rest = rest[0], rest[1:]
    full, sems = rest[-2:]
    outs = rest[:-2]
    me = device_number()
    core = bit_of(me, 0)
    each = a8.shape[0] // (HALF // 2)
    for which, (lower, upper) in enumerate(((a8, r1), (s8, sr1))):
        half = core if which == 0 else 1 - core
        place = own_place(me, orders, half)
        for spot in range(HALF):
            source = lower if spot < HALF // 2 else upper
            begin = (spot % (HALF // 2)) * each
            block = half * HALF + jnp.bitwise_xor(place, spot)
            full[pl.ds(pl.multiple_of(block * each, each), each), :] = source[
                begin : begin + each, :
            ].astype(F32)
    width = full.shape[1]
    copies = []
    if columns:
        out = outs[0]
        for part in range(full.shape[0] // width):
            copies.append(
                pltpu.make_async_copy(
                    full.at[pl.ds(part * width, width), :],
                    out.at[:, pl.ds(part * width, width)],
                    sems.at[part],
                )
            )
    else:
        begin = 0
        count = 0
        for out in outs:
            if len(out.shape) == 2 and out.shape[0] >= width:
                copies.append(
                    pltpu.make_async_copy(full.at[pl.ds(begin, out.shape[0]), :], out, sems.at[count])
                )
                begin += out.shape[0]
                count += 1
    for copy in copies:
        copy.start()
    if with_vec:
        values = vec[...].astype(F32)
        small = [out for out in outs if out.shape[0] == 1]
        for index in range(6):
            small[index][...] = values[index : index + 1, :]
        for part in range(small[6].shape[1] // width):
            small[6][:, part * width : (part + 1) * width] = values[6 + part : 7 + part, :]
    for copy in copies:
        copy.wait()


def call(kernel, name, out_shapes, out_specs, in_specs, scratch, *operands):
    return pl.pallas_call(
        kernel,
        out_shape=out_shapes,
        in_specs=in_specs,
        out_specs=out_specs,
        scratch_shapes=scratch,
        compiler_params=pltpu.CompilerParams(vmem_limit_bytes=50 * 1024 * 1024),
        name=name,
    )(*operands)


def shape(dims, kind=BF):
    return jax.ShapeDtypeStruct(dims, kind)


def per_device(
    row_total,
    tokens, segments, cotangent, query_weight, key_weight, value_weight, out_weight,
    attend_gain, attend_bias, inner_weight, inner_bias, outer_weight, middle_gain, middle_bias,
    adapter_down, adapter_up, joining_query, joining_key, joining_value, final_gain, final_bias,
):
    batches, row_count, length, width = tokens.shape
    here = batches * row_count * length
    hidden_units = inner_weight.shape[1]
    adapters, bottleneck = adapter_up.shape[0], adapter_up.shape[1]
    devices = row_total * 4
    pairs = width // (2 * HEAD)

    def swap(values, partner):
        return lax.ppermute(values, AXES, [(d, partner(d)) for d in range(devices)])

    def over_bit(values, bit):
        return swap(values, lambda d: d ^ (1 << bit))

    def over_stage(values, orders, stage):
        return swap(values, lambda d: d ^ (1 << orders[d & 1][stage]))

    x0 = tokens.reshape(here, width)
    x2 = over_bit(x0, 1)
    x1 = over_bit(x0, 0)
    seg = segments.reshape(batches, length)
    seg_own = jnp.concatenate([seg, over_bit(seg, 1)], 0)
    seg_sib = over_bit(seg_own, 0)
    x3 = over_bit(x2, 0)

    gathered = row_total == 8 and joining_query.shape[0] % 16 == 0
    stacked = jnp.stack([joining_query, joining_key, joining_value], 0)
    if gathered:
        core = lax.rem(lax.axis_index("tok"), 2)
        column = width // 2
        piece = lax.dynamic_slice_in_dim(stacked, core * column, column, 2)[None]
        for stage in range(2):
            piece = jnp.concatenate([piece, over_stage(piece, ORDER_JOIN, stage)], 0)
        upper = over_stage(piece, ORDER_JOIN, 2)
        jw = (piece, upper, over_bit(piece, 0), over_bit(upper, 0))
    else:
        jw = (lax.all_gather(stacked, "rows", axis=1, tiled=True),)

    row = lambda vector: vector.reshape(1, -1)
    (qs, keys, values, probs, attended, n1, rs1, al, active, slope_z, n2, rs2, hidden, bottle, slope_t) = call(
        forward_kernel,
        "forward",
        (
            shape((here, width)), shape((4 * here, width)), shape((4 * here, width)),
            shape((batches * pairs, 4 * length, 2 * length)), shape((here, width)),
            shape((here, width), F32), shape((here, 128), F32), shape((here, width)),
            shape((here, hidden_units)), shape((here, hidden_units)),
            shape((here, width), F32), shape((here, 128), F32), shape((here, width), F32),
            shape((here, width)), shape((here, width)),
        ),
        (VM,) * 15,
        (VM,) * 18,
        [pltpu.VMEM((4 * length, length), F32)],
        x0, x1, x2, x3, seg_own, seg_sib, query_weight, key_weight, value_weight, out_weight,
        inner_weight, outer_weight, adapter_down, row(attend_gain), row(attend_bias), row(inner_bias),
        row(middle_gain), row(middle_bias),
    )

    half_rows = lambda blocks: blocks * width // 2
    up = adapter_up.reshape(adapters * bottleneck, width)
    output, keep_j, send_j, dhp, dt, vec_final = call(
        functools.partial(joining_kernel, gathered, bottleneck, adapters),
        "joining",
        (
            shape((here, width)), shape((half_rows(3), width)), shape((half_rows(3), width)),
            shape((here, width), F32), shape((here, width)), shape((8, width), F32),
        ),
        (VM, ANY, ANY, VM, VM, VM),
        (VM,) * 7 + (ANY,) * len(jw),
        [
            pltpu.VMEM((3, width, width), BF), pltpu.VMEM((3 * width, width), BF),
            pltpu.SemaphoreType.DMA((2, HALF)), pltpu.SemaphoreType.DMA((2, 8)),
        ],
        hidden, bottle, slope_t, up, cotangent.reshape(here, width), row(final_gain), row(final_bias), *jw,
    )

    blocks = hidden_units // width
    d1, vec, keep_u, send_u, keep_i, send_i = call(
        feed_back_kernel,
        "feed_back",
        (
            shape((here, width), F32), shape((16, width), F32),
            shape((half_rows(blocks), width)), shape((half_rows(blocks), width)),
            shape((half_rows(blocks), width)), shape((half_rows(blocks), width)),
        ),
        (VM, VM, ANY, ANY, ANY, ANY),
        (VM,) * 15,
        [
            pltpu.VMEM((blocks * width, width), BF), pltpu.VMEM((blocks * width, width), BF),
            pltpu.SemaphoreType.DMA((2, HALF)), pltpu.SemaphoreType.DMA((2, HALF)),
        ],
        dhp, dt, adapter_down, n2, rs2, row(middle_gain), active, slope_z, inner_weight, outer_weight,
        al, n1, rs1, row(attend_gain), vec_final,
    )

    keep_t, send_t, gi_own, gi_keep, gi_send = call(
        attend_back_kernel,
        "attend_back",
        (
            shape((half_rows(4) + 16, width)), shape((half_rows(4) + 16, width)),
            shape((here, width), F32), shape((here, width)), shape((2 * here, width)),
        ),
        (ANY, ANY, VM, VM, VM),
        (VM,) * 15,
        [
            pltpu.VMEM((4 * width, width), BF), pltpu.VMEM((here, width), BF),
            pltpu.VMEM((4 * here, width), BF), pltpu.VMEM((4 * here, width), BF),
            pltpu.VMEM((here, width), BF), pltpu.VMEM((16, width), BF),
            pltpu.SemaphoreType.DMA((2, HALF)), pltpu.SemaphoreType.DMA((2,)),
        ],
        d1, out_weight, attended, qs, keys, values, probs, x0, x1, x2, x3,
        query_weight, key_weight, value_weight, vec,
    )

    def reduce_scatter(keep, send, orders, rows_each):
        got = over_bit(send, 0)
        rows = HALF * rows_each
        for stage in range(4):
            middle = rows // 2
            send = keep[middle:] + got[middle:]
            keep = jnp.concatenate([keep[:middle] + got[:middle], keep[rows:] + got[rows:]], 0)
            got = over_stage(send, orders, stage)
            rows = middle
        keep = keep + got
        for bit in range(5, devices.bit_length() - 1):
            keep = keep + over_bit(keep, bit)
        return keep

    def all_gather(block, orders):
        for stage in (3, 2, 1):
            block = jnp.concatenate([block, over_stage(block, orders, stage)], 0)
        upper = over_stage(block, orders, 0)
        return block, upper, over_bit(block, 0), over_bit(upper, 0)

    def finish(parts, orders, outs, columns, name, vector=None):
        rows = parts[0].shape[0] * 4
        small = [] if vector is None else [shape((1, width), F32)] * 6 + [shape((1, hidden_units), F32)]
        return call(
            functools.partial(finish_kernel, orders, columns, vector is not None),
            name,
            tuple(outs) + tuple(small),
            (ANY,) * len(outs) + (VM,) * len(small),
            (VM,) * (4 if vector is None else 5),
            [pltpu.VMEM((rows, width), F32), pltpu.SemaphoreType.DMA((4,))],
            *parts, *(() if vector is None else (vector,)),
        )

    square = shape((width, width), F32)
    sum_j = reduce_scatter(keep_j, send_j, ORDER_XY, 3 * width // GROUP)
    sum_u = reduce_scatter(keep_u, send_u, ORDER_XY, blocks * width // GROUP)
    sum_i = reduce_scatter(keep_i, send_i, ORDER_Z, blocks * width // GROUP)
    sum_t = reduce_scatter(keep_t, send_t, ORDER_XY, 4 * width // GROUP)
    each_t = 4 * width // GROUP
    joining = finish(all_gather(sum_j, ORDER_XY), ORDER_XY, [square] * 3, False, "finish_joining")
    outer = finish(
        all_gather(sum_u, ORDER_XY), ORDER_XY, [shape((hidden_units, width), F32)], False, "finish_outer"
    )
    inner = finish(
        all_gather(sum_i, ORDER_Z), ORDER_Z, [shape((width, hidden_units), F32)], True, "finish_inner"
    )
    last = finish(
        all_gather(sum_t[:each_t], ORDER_XY), ORDER_XY, [square] * 4, False, "finish_attend", sum_t[each_t:]
    )

    gi_got = over_bit(gi_send, 0)
    gi_far = over_bit(gi_keep + gi_got[here:], 1)
    input_grad = low(gi_own + gi_got[:here].astype(F32) + gi_far.astype(F32))

    flat = lambda values: values.reshape(-1)
    return (
        output.reshape(tokens.shape), input_grad.reshape(tokens.shape),
        last[0], last[1], last[2], last[3], flat(last[4]), flat(last[5]),
        inner[0], flat(last[10]), outer[0], flat(last[6]), flat(last[7]),
        joining[0], joining[1], joining[2], flat(last[8]), flat(last[9]),
    )


def solution(mesh):
    return jax.shard_map(
        functools.partial(per_device, mesh.shape["rows"]),
        mesh=mesh,
        in_specs=(
            P(None, "rows", "tok", None), P(None, "rows", "tok"), P(None, "rows", "tok", None),
        ) + (P(),) * 13 + (P("rows", None),) * 3 + (P(),) * 2,
        out_specs=(P(None, "rows", "tok", None),) * 2 + (P(),) * 16,
        check_vma=False,
    )
```

```python
import functools

import jax
import jax.numpy as jnp
from jax import lax
from jax.experimental import pallas as pl
from jax.experimental.pallas import tpu as pltpu
from jax.sharding import PartitionSpec as P

HEAD = 64
AXES = ("rows", "tok")
BF = jnp.bfloat16
F32 = jnp.float32
norm_eps = 1e-06

ORDER_XY = ((1, 2, 3, 4), (2, 1, 4, 3))
ORDER_YX = ((2, 1, 3, 4), (1, 2, 4, 3))
ORDER_Z = ((3, 4, 1, 2), (4, 3, 2, 1))
ORDER_ZY = ((4, 3, 1, 2), (3, 4, 2, 1))
ORDERS = {"J": ORDER_XY, "U": ORDER_Z, "I": ORDER_XY, "T": ORDER_XY}
ORDER_JOIN = ((2, 4, 3), (4, 3, 2))
GROUP = 32
THREE = ((0, 1, False), (1, 1, False), (2, 1, False))
PLAN = (
    ("KJ",), ("KU",), ("KI",), ("J", "U",), ("I",), ("KT",), ("J", "U", "I", "T",), ("KG", "I", "U",),
    ("T",), ("I", "J", "g0", "U", "T",), ("I",), ("U", "J",), ("I",), ("U", "T", "J",), ("J",),
    ("I", "U", "T", "g1",), ("J",), ("T",), ("I", "J", "U",), ("T", "I",), ("J", "T",), ("U",),
    ("fI", "fU",), ("T",), ("fJ", "fT",),
)
HALF = GROUP // 2

VM = pl.BlockSpec(memory_space=pltpu.VMEM)
ANY = pl.BlockSpec(memory_space=pl.ANY)


def dot(left, right):
    return jnp.dot(left, right, preferred_element_type=F32)


def dot_tn(left, right):
    return lax.dot_general(left, right, (((0,), (0,)), ((), ())), preferred_element_type=F32)


def dot_nt(left, right):
    return lax.dot_general(left, right, (((1,), (1,)), ((), ())), preferred_element_type=F32)


def low(values):
    return values.astype(BF)


def normalize(values, gain, shift):
    centered = values - jnp.mean(values, -1, keepdims=True)
    inv_std = lax.rsqrt(jnp.mean(centered * centered, -1, keepdims=True) + norm_eps)
    unit = centered * inv_std
    return unit * gain + shift, unit, inv_std


def normalize_back(upstream, unit, inv_std, gain):
    grad_unit = upstream * gain
    projected = grad_unit - jnp.mean(grad_unit, -1, keepdims=True)
    projected = projected - unit * jnp.mean(grad_unit * unit, -1, keepdims=True)
    gain_term = jnp.sum(upstream * unit, 0, keepdims=True)
    return projected * inv_std, gain_term, jnp.sum(upstream, 0, keepdims=True)


def gelu_both(values):
    normal_cdf = 0.5 * (1.0 + lax.erf(values * 0.7071067811865476))
    slope = normal_cdf + values * jnp.exp(-0.5 * values * values) * 0.3989422804014327
    return values * normal_cdf, slope


def device_number():
    return lax.axis_index("rows") * 4 + lax.axis_index("tok")


def bit_of(number, bit):
    return lax.rem(lax.div(number, 1 << bit), 2)


def own_place(number, orders, core):
    def along(order):
        total = 0
        for bit in order:
            total = total * 2 + bit_of(number, bit)
        return total

    return jnp.where(core == 0, along(orders[0]), along(orders[1]))


def put_blocks(target, values, first_row, place, rows_each):
    row = first_row
    while row < first_row + values.shape[0]:
        block, within = divmod(row, rows_each)
        count = min(rows_each - within, first_row + values.shape[0] - row)
        spot = jnp.bitwise_xor(place, block) * rows_each + within
        target[pl.ds(pl.multiple_of(spot, 16), count), :] = values[row - first_row : row - first_row + count, :]
        row += count


def halves(keep, send, orders):
    me = device_number()
    core = bit_of(me, 0)
    return (
        (keep, core, own_place(me, orders, core)),
        (send, 1 - core, own_place(me, orders, 1 - core)),
    )


def half_columns(ref, half, begin=0, count=None):
    size = ref.shape[1] // 2
    count = size if count is None else count
    return ref[:, pl.ds(pl.multiple_of(half * size + begin, 128), count)]


def of_bank(bank, index):
    width = bank.shape[0]
    return bank[:, index * width : (index + 1) * width]


def row_slices(ref, batch, length, lanes):
    here = ref.shape[0] // 4
    begins = [place * here + batch * length for place in range(4)]
    return jnp.concatenate([ref[begin : begin + length, lanes] for begin in begins], 0)


def attend_kernel(
    x01, x2, x3, seg0, seg1, seg2, seg3, bank, ag, ab,
    qs_ref, k_ref, v_ref, p_ref, o_ref, n1_ref, rs1_ref, bias,
):
    tokens_here, width = x2.shape
    batches = seg0.shape[0]
    length = tokens_here // batches
    qs_ref[...] = low(low(dot(x01[:tokens_here, :], of_bank(bank, 0))) * HEAD ** (-0.5))
    row = 0
    for piece in (x01, x2, x3):
        span = slice(row, row + piece.shape[0])
        k_ref[span, :] = low(dot(piece[...], of_bank(bank, 1)))
        v_ref[span, :] = low(dot(piece[...], of_bank(bank, 2)))
        row += piece.shape[0]
    segments = [ref[...].astype(F32) for ref in (seg0, seg1, seg2, seg3)]
    lane = lax.broadcasted_iota(jnp.int32, (1, 2 * HEAD), 1)
    first = (lane < HEAD).astype(BF)
    second = (lane >= HEAD).astype(BF)
    for batch in range(batches):
        query_seg = segments[0][batch : batch + 1, :]
        for index, segment in enumerate(segments):
            row = segment[batch : batch + 1, :]
            key_seg = jnp.transpose(jnp.broadcast_to(row, (length, length)))
            bias[pl.ds(index * length, length), :] = jnp.where(key_seg == query_seg, 0.0, -1e30)
        both = jnp.concatenate([bias[...], bias[...]], 1)
        for pair in range(width // (2 * HEAD)):
            lanes = slice(pair * 2 * HEAD, (pair + 1) * 2 * HEAD)
            kp = row_slices(k_ref, batch, length, lanes)
            vp = row_slices(v_ref, batch, length, lanes)
            qp = qs_ref[batch * length : (batch + 1) * length, lanes]
            stacked = jnp.concatenate([qp * first, qp * second], 0)
            scores = dot_nt(kp, stacked) + both
            exps = jnp.exp(scores - jnp.max(scores, 0, keepdims=True))
            probs = low(exps * (1.0 / jnp.sum(exps, 0, keepdims=True)))
            p_ref[batch * (width // (2 * HEAD)) + pair] = probs
            mixed = dot_tn(vp, probs)
            joined = jnp.concatenate([mixed[:HEAD, :length], mixed[HEAD:, length:]], 0)
            o_ref[batch * length : (batch + 1) * length, lanes] = low(jnp.transpose(joined))
    residual = x01[:tokens_here, :].astype(F32) + dot(o_ref[...], of_bank(bank, 3))
    _, unit, inv_std = normalize(residual, ag[...], ab[...])
    n1_ref[...] = unit
    rs1_ref[...] = jnp.broadcast_to(inv_std, rs1_ref.shape)


def feed_kernel(
    n1_ref, ag, ab, wi, bi, wu, mg, mb, bank, u_ref, sz_ref, n2_ref, rs2_ref, c_ref, st_ref
):
    width = n1_ref.shape[1]
    outer = n1_ref[...] * ag[...] + ab[...]
    al = low(outer)
    for part in range(wi.shape[1] // width):
        span = slice(part * width, (part + 1) * width)
        inner = dot(al, wi[:, span]) + bi[:, span]
        active, slope = gelu_both(inner)
        u_ref[:, span] = low(active)
        sz_ref[:, span] = low(slope)
        outer = outer + dot(low(active), wu[span, :])
    hidden, unit, inv_std = normalize(outer, mg[...], mb[...])
    n2_ref[...] = unit
    rs2_ref[...] = jnp.broadcast_to(inv_std, rs2_ref.shape)
    active, slope = gelu_both(dot(low(hidden), of_bank(bank, 4)))
    c_ref[...] = low(active)
    st_ref[...] = low(slope)


def joining_kernel(
    gathered, bottleneck, adapters, n2_ref, mg, mb, c_ref, st_ref, up, cot, fg, fb, *rest
):
    if gathered:
        jw_in, rest = rest[:8], rest[8:]
    else:
        jw_in, rest = rest[:1], rest[1:]
    out_ref, keep, send, dhp_ref, dt_ref, vec_ref, wj, left, right = rest
    width = n2_ref.shape[1]
    scale = width ** (-0.5)
    me = device_number()
    core = bit_of(me, 0)
    if gathered:
        shard, column = jw_in[0].shape[2:]
        for which in range(2):
            half = core if which == 0 else 1 - core
            columns = pl.ds(pl.multiple_of(half * column, column), column)
            for spot in range(8):
                flips = [sum(((spot >> i) & 1) << (order[i] - 2) for i in range(3)) for order in ORDER_JOIN]
                owner = jnp.bitwise_xor(lax.div(me, 4), jnp.where(half == 0, flips[0], flips[1]))
                rows = pl.ds(pl.multiple_of(owner * shard, shard), shard)
                for matrix in range(3):
                    wj[matrix, rows, columns] = jw_in[which * 4 + spot // 2][spot % 2, matrix]
    else:
        wj[...] = jw_in[0][...]
    hidden = n2_ref[...] * mg[...] + mb[...]
    hidden_low = low(hidden)
    cf = c_ref[...].astype(F32)
    row_group = lax.broadcasted_iota(jnp.int32, (width, 128), 0) // bottleneck
    column_of = lax.broadcasted_iota(jnp.int32, (width, 128), 1)
    member = (row_group == column_of).astype(BF)
    valid = lax.broadcasted_iota(jnp.int32, (1, 128), 1) < adapters

    def per_adapter(values):
        high = low(values)
        rest_of = low(values - high.astype(F32))
        return dot(high, member) + dot(rest_of, member)

    fq = low(dot(hidden_low, wj[0]))
    probe = low(dot_nt(fq, wj[1]))
    probe_f = probe.astype(F32)
    up_probe = dot_nt(probe, up[...])
    scores = (
        per_adapter(cf * up_probe) + jnp.sum(hidden * probe_f, -1, keepdims=True)
    ) * scale
    scores = jnp.where(valid, scores, -1e30)
    exps = jnp.exp(scores - jnp.max(scores, -1, keepdims=True))
    weights = exps * (1.0 / jnp.sum(exps, -1, keepdims=True))
    weights_low = low(weights)
    weights_wide = dot_nt(weights_low, member)
    weights_sum = jnp.sum(weights_low.astype(F32), -1, keepdims=True)
    mixed = low(weights_sum * hidden + dot(low(weights_wide * cf), up[...]))
    final, unit, inv_std = normalize(hidden + dot(mixed, wj[2]), fg[...], fb[...])
    out_ref[...] = low(final)
    d3, gain_term, shift_term = normalize_back(cot[...].astype(F32), unit, inv_std, fg[...])
    vec_ref[...] = jnp.concatenate(
        [gain_term, shift_term, jnp.zeros((vec_ref.shape[0] - 2, width), F32)], 0
    )
    dfo = low(d3)
    left[2] = mixed
    right[2] = dfo
    dm = low(dot_nt(dfo, wj[2]))
    dm_f = dm.astype(F32)
    up_dm = dot_nt(dm, up[...])
    dw = per_adapter(cf * up_dm) + jnp.sum(hidden * dm_f, -1, keepdims=True)
    df = low(weights * (dw - jnp.sum(weights * dw, -1, keepdims=True)))
    df_wide = dot_nt(df, member)
    df_sum = jnp.sum(df.astype(F32), -1, keepdims=True)
    dr = low((df_sum * hidden + dot(low(df_wide * cf), up[...])) * scale)
    left[1] = dr
    right[1] = fq
    dfq = low(dot(dr, wj[1]))
    left[0] = hidden_low
    right[0] = dfq
    for target, half, place in halves(keep, send, ORDERS["J"]):
        for matrix in range(3):
            term = low(dot_tn(half_columns(left.at[matrix], half), right[matrix]))
            put_blocks(target, term, matrix * (width // 2), place, 3 * width // GROUP)
    dc = weights_wide * up_dm + (df_wide * scale) * up_probe
    dt_ref[...] = low(dc * st_ref[...].astype(F32))
    dhp_ref[...] = (
        d3 + weights_sum * dm_f + (df_sum * scale) * probe_f + dot_nt(dfq, wj[0])
    )


def outer_back_kernel(
    dhp_ref, dt_ref, bank, n2_ref, rs2_ref, mg, u_ref, d2_ref, vec_ref, keep, send
):
    width = dhp_ref.shape[1]
    hidden_grad = dhp_ref[...] + dot_nt(dt_ref[...], of_bank(bank, 4))
    d2, mg_term, mb_term = normalize_back(hidden_grad, n2_ref[...], rs2_ref[:, :1], mg[...])
    d2_ref[...] = d2
    dfw = low(d2)
    units = u_ref.shape[1]
    for target, half, place in halves(keep, send, ORDERS["U"]):
        for begin in range(0, units // 2, width):
            term = low(dot_tn(half_columns(u_ref, half, begin, width), dfw))
            put_blocks(target, term, begin, place, units // GROUP)
    vec_ref[...] = jnp.concatenate([mg_term, mb_term, jnp.zeros((vec_ref.shape[0] - 2, width), F32)], 0)


def inner_back_kernel(
    d2_ref, sz_ref, wi, wu, n1_ref, rs1_ref, ag, ab, o_ref, vec_final, vec_middle,
    d1_ref, vec_ref, keep, send, dz_scr, dao_scr,
):
    width = d2_ref.shape[1]
    total = d2_ref[...]
    dfw = low(total)
    al = low(n1_ref[...] * ag[...] + ab[...])
    bias_terms = []
    parts = wi.shape[1] // width
    for part in range(parts):
        span = slice(part * width, (part + 1) * width)
        dz = low(dot_nt(dfw, wu[span, :]) * sz_ref[:, span].astype(F32))
        bias_terms.append(jnp.sum(dz.astype(F32), 0, keepdims=True))
        dz_scr[:, span] = dz
        total = total + dot_nt(dz, wi[:, span])
    d1, ag_term, ab_term = normalize_back(total, n1_ref[...], rs1_ref[:, :1], ag[...])
    d1_ref[...] = d1
    dao_scr[...] = low(d1)
    units = wi.shape[1]
    rows_each = (units + width) // GROUP
    for target, half, place in halves(keep, send, ORDERS["I"]):
        for begin in range(0, units // 2, width):
            term = low(dot_tn(al, half_columns(dz_scr, half, begin, width)))
            put_blocks(target, term, begin, place, rows_each)
        term = low(dot_tn(half_columns(o_ref, half), dao_scr[...]))
        put_blocks(target, term, units // 2, place, rows_each)
    rows = [ag_term, ab_term, vec_middle[0:1, :], vec_middle[1:2, :], vec_final[0:1, :], vec_final[1:2, :]]
    rows += bias_terms
    rows.append(jnp.zeros((vec_ref.shape[0] - len(rows), width), F32))
    vec_ref[...] = low(jnp.concatenate(rows, 0))


def attend_back_kernel(
    d1_ref, bank, o_ref, qs_ref, k_ref, v_ref, p_ref, x01, x2, x3, vec_ref,
    keep, send, dq_ref, dk_ref, dv_ref, do_scr, row_x,
):
    tokens_here, width = x2.shape
    length = p_ref.shape[2] // 2
    batches = tokens_here // length
    pairs = width // (2 * HEAD)
    do_scr[...] = low(dot_nt(low(d1_ref[...]), of_bank(bank, 3)))
    lane = lax.broadcasted_iota(jnp.int32, (1, 2 * HEAD), 1)
    first = (lane < HEAD).astype(BF)
    second = (lane >= HEAD).astype(BF)
    for batch in range(batches):
        here = slice(batch * length, (batch + 1) * length)
        spans = [
            slice(index * tokens_here + batch * length, index * tokens_here + (batch + 1) * length)
            for index in range(4)
        ]
        for pair in range(pairs):
            lanes = slice(pair * 2 * HEAD, (pair + 1) * 2 * HEAD)
            kp = row_slices(k_ref, batch, length, lanes)
            vp = row_slices(v_ref, batch, length, lanes)
            qp = qs_ref[here, lanes]
            dop = do_scr[here, lanes]
            q_stacked = jnp.concatenate([qp * first, qp * second], 0)
            do_stacked = jnp.concatenate([dop * first, dop * second], 0)
            probs = p_ref[batch * pairs + pair]
            op = o_ref[here, lanes].astype(F32)
            product = dop.astype(F32) * op
            high = low(product)
            rest = low(product - high.astype(F32))
            spread = jnp.concatenate([high * first, high * second], 0)
            spread_rest = jnp.concatenate([rest * first, rest * second], 0)
            ones = jnp.ones((8, 2 * HEAD), BF)
            shift = (dot_nt(ones, spread) + dot_nt(ones, spread_rest))[:1, :]
            ds = low(probs.astype(F32) * (dot_nt(vp, do_stacked) - shift))
            dv = low(dot(probs, do_stacked))
            dk = low(dot(ds, q_stacked))
            for index, span in enumerate(spans):
                rows = slice(index * length, (index + 1) * length)
                dk_ref[span, lanes] = dk[rows, :]
                dv_ref[span, lanes] = dv[rows, :]
            mixed = dot_tn(kp, ds)
            joined = jnp.concatenate([mixed[:HEAD, :length], mixed[HEAD:, length:]], 0)
            dq_ref[here, lanes] = low(jnp.transpose(joined) * HEAD ** (-0.5))
    row_x[: 2 * tokens_here, :] = x01[...]
    row_x[2 * tokens_here : 3 * tokens_here, :] = x2[...]
    row_x[3 * tokens_here :, :] = x3[...]
    rows_each = 3 * width // GROUP
    for target, half, place in halves(keep, send, ORDERS["T"]):
        terms = (
            dot_tn(half_columns(x01.at[:tokens_here, :], half), dq_ref[...]),
            dot_tn(half_columns(row_x, half), dk_ref[...]),
            dot_tn(half_columns(row_x, half), dv_ref[...]),
        )
        for matrix, term in enumerate(terms):
            put_blocks(target, low(term), matrix * (width // 2), place, rows_each)
        target[HALF * rows_each :, :] = vec_ref[...]


def input_back_kernel(d1_ref, dq_ref, dk_ref, dv_ref, bank, gi_own, gi_keep, gi_send):
    tokens_here = d1_ref.shape[0]
    parts = []
    for index in range(4):
        span = slice(index * tokens_here, (index + 1) * tokens_here)
        parts.append(dot_nt(dk_ref[span, :], of_bank(bank, 1)) + dot_nt(dv_ref[span, :], of_bank(bank, 2)))
    gi_own[...] = parts[0] + d1_ref[...] + dot_nt(dq_ref[...], of_bank(bank, 0))
    gi_keep[...] = low(parts[2])
    gi_send[:tokens_here, :] = low(parts[1])
    gi_send[tokens_here:, :] = low(parts[3])


def finish_kernel(orders, layout, with_vec, a8, r1, s8, sr1, *rest):
    if with_vec:
        vec, rest = rest[0], rest[1:]
    full, sems = rest[-2:]
    outs = rest[:-2]
    me = device_number()
    core = bit_of(me, 0)
    each = a8.shape[0] // (HALF // 2)
    half_rows = HALF * each
    width = full.shape[1]
    copies = []
    for which, (lower, upper) in enumerate(((a8, r1), (s8, sr1))):
        half = core if which == 0 else 1 - core
        place = own_place(me, orders, half)
        base = pl.multiple_of(half * half_rows, half_rows)
        for spot in range(HALF):
            source = lower if spot < HALF // 2 else upper
            begin = (spot % (HALF // 2)) * each
            block = jnp.bitwise_xor(place, spot)
            full[pl.ds(pl.multiple_of(base + block * each, 8), each), :] = source[
                begin : begin + each, :
            ].astype(F32)
        row = 0
        for out, pieces, by_column in layout:
            for piece in range(pieces):
                target = outs[out]
                if by_column:
                    size = target.shape[0]
                    column = pl.multiple_of((half * pieces + piece) * width, width)
                    target = target.at[:, pl.ds(column, width)]
                else:
                    size = target.shape[0] // 2
                    target = target.at[pl.ds(pl.multiple_of(half * size, size), size), :]
                source = full.at[pl.ds(pl.multiple_of(base + row, 8), size), :]
                copies.append(pltpu.make_async_copy(source, target, sems.at[len(copies)]))
                copies[-1].start()
                row += size
    if with_vec:
        values = vec[...].astype(F32)
        small = [out for out in outs if out.shape[0] == 1]
        for index in range(6):
            small[index][...] = values[index : index + 1, :]
        for part in range(small[6].shape[1] // width):
            small[6][:, part * width : (part + 1) * width] = values[6 + part : 7 + part, :]
    for copy in copies:
        copy.wait()


def call(kernel, name, microseconds, out_shapes, out_specs, in_specs, scratch, *operands):
    return pl.pallas_call(
        kernel,
        out_shape=out_shapes,
        in_specs=in_specs,
        out_specs=out_specs,
        scratch_shapes=scratch,
        compiler_params=pltpu.CompilerParams(vmem_limit_bytes=32 * 1024 * 1024),
        cost_estimate=pl.CostEstimate(
            flops=int(microseconds * 1e4), bytes_accessed=int(microseconds * 1e2), transcendentals=0
        ),
        name=name,
    )(*operands)


def shape(dims, kind=BF):
    return jax.ShapeDtypeStruct(dims, kind)


def per_device(
    row_total,
    tokens, segments, cotangent, query_weight, key_weight, value_weight, out_weight,
    attend_gain, attend_bias, inner_weight, inner_bias, outer_weight, middle_gain, middle_bias,
    adapter_down, adapter_up, joining_query, joining_key, joining_value, final_gain, final_bias,
):
    batches, row_count, length, width = tokens.shape
    here = batches * row_count * length
    hidden_units = inner_weight.shape[1]
    adapters, bottleneck = adapter_up.shape[0], adapter_up.shape[1]
    devices = row_total * 4
    pairs = width // (2 * HEAD)

    def swap(values, partner):
        return lax.ppermute(values, AXES, [(d, partner(d)) for d in range(devices)])

    def over_bit(values, bit, label="over_bit"):
        with jax.named_scope(label):
            return swap(values, lambda d: d ^ (1 << bit))

    def over_stage(values, orders, stage, label="over_stage"):
        with jax.named_scope(label):
            return swap(values, lambda d: d ^ (1 << orders[d & 1][stage]))

    token = [lax.create_token()]

    def gate(values):
        return lax.optimization_barrier((token[0], values))[1]

    def mark(values):
        token[0], values = lax.optimization_barrier((token[0], values))
        return values

    row = lambda vector: vector.reshape(1, -1)

    gathered = row_total == 8 and joining_query.shape[0] % 16 == 0
    stacked = jnp.stack([joining_query, joining_key, joining_value], 0)
    if gathered:
        core = lax.rem(lax.axis_index("tok"), 2)
        column = width // 2
        piece = lax.dynamic_slice_in_dim(stacked, core * column, column, 2)[None]
        far = over_stage(piece, ORDER_JOIN, 0, "weights_first")

    x0 = tokens.reshape(here, width)
    x2 = over_bit(x0, 1, "row_far")
    x1 = over_bit(x0, 0, "row_near")
    seg = segments.reshape(batches, length)
    with jax.named_scope("segments"):
        segs = [seg] + [swap(seg, lambda d, flip=flip: d ^ flip) for flip in (1, 2, 3)]
    if gathered:
        far = mark(far)
    if gathered:
        near = mark(jnp.concatenate([piece, gate(far)], 0))
        far = over_stage(near, ORDER_JOIN, 1, "weights_second")
    bank = mark(
        jnp.concatenate([gate(query_weight), key_weight, value_weight, out_weight, adapter_down], 1)
    )
    x01 = mark(jnp.concatenate([x0, gate(x1)], 0))
    segs = mark(segs)
    x2 = mark(x2)
    x3 = over_bit(x2, 0, "row_cross")
    if gathered:
        far = mark(far)
        third = [over_stage(part, ORDER_JOIN, 2, "weights_third") for part in (near, far)]
    else:
        jw = (lax.all_gather(stacked, "rows", axis=1, tiled=True),)

    x3 = mark(x3)
    qs, keys, values, probs, attended, n1, rs1 = call(
        attend_kernel,
        "attend",
        6,
        (
            shape((here, width)), shape((4 * here, width)), shape((4 * here, width)),
            shape((batches * pairs, 4 * length, 2 * length)), shape((here, width)),
            shape((here, width), F32), shape((here, 128), F32),
        ),
        (VM,) * 7,
        (VM,) * 10,
        [pltpu.VMEM((4 * length, length), F32)],
        x01, x2, x3, *segs, bank,
        gate(row(attend_gain)), row(attend_bias),
    )
    if gathered:
        n1 = mark(n1)
        third = mark(third)
        jw = (near, far, *third)
        jw += tuple(over_bit(gate(part), 0, "weights_core") for part in jw)
    active, slope_z, n2, rs2, bottle, slope_t = call(
        feed_kernel,
        "feed",
        3,
        (
            shape((here, hidden_units)), shape((here, hidden_units)), shape((here, width), F32),
            shape((here, 128), F32), shape((here, width)), shape((here, width)),
        ),
        (VM,) * 6,
        (VM,) * 9,
        [],
        n1, row(attend_gain), row(attend_bias), inner_weight, row(inner_bias), outer_weight,
        gate(row(middle_gain)), row(middle_bias), bank,
    )
    n2 = mark(n2)

    waiting = []

    def later(values, travel, put):
        waiting.append((values, travel, put, len(waiting)))

    def start_waiting():
        for values, travel, put, place in waiting:
            put(travel(values if place == len(waiting) - 1 else gate(values)))
        waiting.clear()

    class Stream:
        def __init__(self, name, orders, rows_each):
            self.name, self.orders, self.rows_each, self.count = name, orders, rows_each, 0

        def send(self, values, stage, label, into="got"):
            def travel(operand):
                with jax.named_scope(f"{self.name}_{label}"):
                    if stage is None:
                        return over_bit(operand, 0)
                    return over_stage(operand, self.orders, stage)

            later(values, travel, lambda result: setattr(self, into, result))

        def begin(self, keep, send):
            self.keep, self.rows = keep, HALF * self.rows_each
            self.send(mark(send), None, "core")

        def step(self):
            stage, self.count = self.count, self.count + 1
            label = f"step_{stage}"
            keep, got = self.keep, gate(self.got)
            if stage < 4:
                middle = self.rows // 2
                send = mark(keep[middle:] + got[middle:])
                self.send(send, stage, label)
                self.keep = jnp.concatenate(
                    [keep[:middle] + got[:middle], keep[self.rows :] + got[self.rows :]], 0
                )
                self.rows = middle
            elif stage == 4:
                block = keep + got
                for bit in range(5, devices.bit_length() - 1):
                    block = block + over_bit(block, bit)
                self.extra = block[self.rows_each :]
                self.keep = mark(block[: self.rows_each])
                self.send(self.keep, 3, label)
            elif stage < 8:
                self.keep = mark(jnp.concatenate([keep, got], 0))
                self.send(self.keep, 7 - stage, label)
                if stage == 7:
                    self.send(self.keep, None, "sibling", "sibling")
            else:
                self.got, self.sibling = mark((got, self.sibling))
                self.send(self.got, None, "upper", "upper")

        def parts(self):
            return self.keep, self.got, self.sibling, self.upper

    def finish(stream, outs, layout, name, vector=None):
        parts = stream.parts()
        rows = parts[0].shape[0] * 4
        small = [] if vector is None else [shape((1, width), F32)] * 6 + [shape((1, hidden_units), F32)]
        out = call(
            functools.partial(finish_kernel, stream.orders, layout, vector is not None),
            name,
            2,
            tuple(outs) + tuple(small),
            (ANY,) * len(outs) + (VM,) * len(small),
            (VM,) * (4 if vector is None else 5),
            [pltpu.VMEM((rows, width), F32), pltpu.SemaphoreType.DMA((8,))],
            parts[0], parts[1], parts[2], gate(parts[3]), *(() if vector is None else (vector,)),
        )
        out = list(out)
        out[0] = mark(out[0])
        return out

    blocks = hidden_units // width
    square = shape((width, width), F32)
    each = lambda count: count * width // GROUP
    streams = {
        "J": Stream("joining_sum", ORDERS["J"], each(3)),
        "U": Stream("outer_sum", ORDERS["U"], each(blocks)),
        "I": Stream("inner_sum", ORDERS["I"], each(blocks + 1)),
        "T": Stream("attend_sum", ORDERS["T"], each(3)),
    }
    done = {}

    half_rows = lambda count: count * width // 2
    up = adapter_up.reshape(adapters * bottleneck, width)

    def joining_step():
        done["output"], keep, send, done["dhp"], done["dt"], done["vec_final"] = call(
            functools.partial(joining_kernel, gathered, bottleneck, adapters),
            "joining",
            8,
            (
                shape((here, width)), shape((half_rows(3), width)), shape((half_rows(3), width)),
                shape((here, width), F32), shape((here, width)), shape((8, width), F32),
            ),
            (VM,) * 6,
            (VM,) * (9 + len(jw)),
            [
                pltpu.VMEM((3, width, width), BF), pltpu.VMEM((3, here, width), BF),
                pltpu.VMEM((3, here, width), BF),
            ],
            n2, row(middle_gain), row(middle_bias), bottle, slope_t, up, cotangent.reshape(here, width),
            row(final_gain), row(final_bias), *jw,
        )
        streams["J"].begin(keep, send)

    def outer_step():
        done["d2"], done["vec_middle"], keep, send = call(
            outer_back_kernel,
            "outer_back",
            4,
            (
                shape((here, width), F32), shape((8, width), F32),
                shape((half_rows(blocks), width)), shape((half_rows(blocks), width)),
            ),
            (VM,) * 4,
            (VM,) * 7,
            [],
            done["dhp"], done["dt"], bank, n2, rs2, gate(row(middle_gain)), active,
        )
        streams["U"].begin(keep, send)

    def inner_step():
        done["d1"], done["vec"], keep, send = call(
            inner_back_kernel,
            "inner_back",
            6,
            (
                shape((here, width), F32), shape((16, width)),
                shape((half_rows(blocks + 1), width)), shape((half_rows(blocks + 1), width)),
            ),
            (VM,) * 4,
            (VM,) * 11,
            [pltpu.VMEM((here, hidden_units), BF), pltpu.VMEM((here, width), BF)],
            done["d2"], slope_z, inner_weight, outer_weight, n1, rs1, gate(row(attend_gain)),
            row(attend_bias), attended, done["vec_final"], done["vec_middle"],
        )
        streams["I"].begin(keep, send)

    def attend_step():
        keep, send, done["dq"], done["dk"], done["dv"] = call(
            attend_back_kernel,
            "attend_back",
            8,
            (
                shape((half_rows(3) + 16, width)), shape((half_rows(3) + 16, width)),
                shape((here, width)), shape((4 * here, width)), shape((4 * here, width)),
            ),
            (VM,) * 5,
            (VM,) * 11,
            [pltpu.VMEM((here, width), BF), pltpu.VMEM((4 * here, width), BF)],
            done["d1"], bank, attended, qs, keys, values, probs, x01, x2, x3, gate(done["vec"]),
        )
        streams["T"].begin(keep, send)

    def input_step():
        own, keep, send = call(
            input_back_kernel,
            "input_back",
            2,
            (shape((here, width), F32), shape((here, width)), shape((2 * here, width))),
            (VM,) * 3,
            (VM,) * 5,
            [],
            gate(done["d1"]), done["dq"], done["dk"], done["dv"], bank,
        )
        keep = mark(keep)
        done["gi"] = (own, keep)
        later(send, lambda values: over_bit(values, 0), lambda result: done.update(near=result))

    kernels = {"KJ": joining_step, "KU": outer_step, "KI": inner_step, "KT": attend_step, "KG": input_step}

    def run(plan):
        for step in [step for group in plan for step in group + (None,)]:
            if step is None:
                start_waiting()
            elif step in kernels:
                kernels[step]()
            elif step == "fJ":
                done["J"] = finish(streams["J"], [square] * 3, THREE, "finish_joining")
            elif step == "fU":
                done["U"] = finish(
                    streams["U"], [shape((hidden_units, width), F32)], ((0, 1, False),), "finish_outer"
                )
            elif step == "fI":
                done["I"] = finish(
                    streams["I"], [shape((width, hidden_units), F32), square],
                    ((0, blocks // 2, True), (1, 1, False)), "finish_inner",
                )
            elif step == "fT":
                done["T"] = finish(streams["T"], [square] * 3, THREE, "finish_attend", streams["T"].extra)
            elif step == "g0":
                got = gate(done["near"])
                send = mark(done["gi"][1] + got[here:])
                later(send, lambda values: over_bit(values, 1), lambda result: done.update(far=result))
                done["near"] = got[:here]
            elif step == "g1":
                far = gate(done["far"])
                done["input"] = mark(low(done["gi"][0] + done["near"].astype(F32) + far.astype(F32)))
            else:
                streams[step].step()

    run(PLAN)
    last, inner, out_grad = done["T"], done["I"][0], done["I"][1]
    outer, joining, output, input_grad = done["U"][0], done["J"], done["output"], done["input"]
    flat = lambda values: values.reshape(-1)
    return (
        output.reshape(tokens.shape), input_grad.reshape(tokens.shape),
        last[0], last[1], last[2], out_grad, flat(last[3]), flat(last[4]),
        inner, flat(last[9]), outer, flat(last[5]), flat(last[6]),
        joining[0], joining[1], joining[2], flat(last[7]), flat(last[8]),
    )


def solution(mesh):
    return jax.shard_map(
        functools.partial(per_device, mesh.shape["rows"]),
        mesh=mesh,
        in_specs=(
            P(None, "rows", "tok", None), P(None, "rows", "tok"), P(None, "rows", "tok", None),
        ) + (P(),) * 13 + (P("rows", None),) * 3 + (P(),) * 2,
        out_specs=(P(None, "rows", "tok", None),) * 2 + (P(),) * 16,
        check_vma=False,
    )
```

```python
import functools

import jax
import jax.numpy as jnp
from jax import lax
from jax.experimental import pallas as pl
from jax.experimental.pallas import tpu as pltpu
from jax.sharding import PartitionSpec as P

HEAD = 64
AXES = ("rows", "tok")
BF = jnp.bfloat16
F32 = jnp.float32
norm_eps = 1e-06

ORDER_XY = ((1, 2, 3, 4), (2, 1, 3, 4))
ORDER_YX = ((2, 1, 3, 4), (1, 2, 3, 4))
ORDER_Z = ((3, 4, 1, 2), (4, 3, 2, 1))
ORDER_ZY = ((4, 3, 1, 2), (3, 4, 2, 1))
ORDERS = {"J": ORDER_XY, "U": ORDER_Z, "I": ORDER_XY, "T": ORDER_XY}
ORDER_JOIN = ((2, 4, 3), (4, 3, 2))
GROUP = 32
THREE = ((0, 1, False), (1, 1, False), (2, 1, False))
PLAN = (
    ("KJ",), ("KU",), ("KI",), ("J", "U",), ("I",), ("KT",), ("J", "U", "I", "T",), ("KG", "I", "U",),
    ("T",), ("I", "J", "g0", "U", "T",), ("I",), ("U", "J",), ("I",), ("U", "T", "J",), ("J",),
    ("I", "U", "T", "g1",), ("J",), ("T",), ("I", "J", "U",), ("T", "I",), ("J", "T",), ("U",),
    ("fI", "fU", "fJ",), ("T",), ("hT",), ("fT",),
)
HALF = GROUP // 2

VM = pl.BlockSpec(memory_space=pltpu.VMEM)
ANY = pl.BlockSpec(memory_space=pl.ANY)


def dot(left, right):
    return jnp.dot(left, right, preferred_element_type=F32)


def dot_tn(left, right):
    return lax.dot_general(left, right, (((0,), (0,)), ((), ())), preferred_element_type=F32)


def dot_nt(left, right):
    return lax.dot_general(left, right, (((1,), (1,)), ((), ())), preferred_element_type=F32)


def low(values):
    return values.astype(BF)


def normalize(values, gain, shift):
    centered = values - jnp.mean(values, -1, keepdims=True)
    inv_std = lax.rsqrt(jnp.mean(centered * centered, -1, keepdims=True) + norm_eps)
    unit = centered * inv_std
    return unit * gain + shift, unit, inv_std


def normalize_back(upstream, unit, inv_std, gain):
    grad_unit = upstream * gain
    projected = grad_unit - jnp.mean(grad_unit, -1, keepdims=True)
    projected = projected - unit * jnp.mean(grad_unit * unit, -1, keepdims=True)
    gain_term = jnp.sum(upstream * unit, 0, keepdims=True)
    return projected * inv_std, gain_term, jnp.sum(upstream, 0, keepdims=True)


def gelu_both(values):
    normal_cdf = 0.5 * (1.0 + lax.erf(values * 0.7071067811865476))
    slope = normal_cdf + values * jnp.exp(-0.5 * values * values) * 0.3989422804014327
    return values * normal_cdf, slope


def device_number():
    return lax.axis_index("rows") * 4 + lax.axis_index("tok")


def bit_of(number, bit):
    return lax.rem(lax.div(number, 1 << bit), 2)


def own_place(number, orders, core):
    def along(order):
        total = 0
        for bit in order:
            total = total * 2 + bit_of(number, bit)
        return total

    return jnp.where(core == 0, along(orders[0]), along(orders[1]))


def put_blocks(target, values, first_row, place, rows_each):
    row = first_row
    while row < first_row + values.shape[0]:
        block, within = divmod(row, rows_each)
        count = min(rows_each - within, first_row + values.shape[0] - row)
        spot = jnp.bitwise_xor(place, block) * rows_each + within
        target[pl.ds(pl.multiple_of(spot, 16), count), :] = values[row - first_row : row - first_row + count, :]
        row += count


def halves(keep, send, orders):
    me = device_number()
    core = bit_of(me, 0)
    return (
        (keep, core, own_place(me, orders, core)),
        (send, 1 - core, own_place(me, orders, 1 - core)),
    )


def half_columns(ref, half, begin=0, count=None):
    size = ref.shape[1] // 2
    count = size if count is None else count
    return ref[:, pl.ds(pl.multiple_of(half * size + begin, 128), count)]


def of_bank(bank, index):
    width = bank.shape[0]
    return bank[:, index * width : (index + 1) * width]


def row_slices(ref, batch, length, lanes):
    here = ref.shape[0] // 4
    begins = [place * here + batch * length for place in range(4)]
    return jnp.concatenate([ref[begin : begin + length, lanes] for begin in begins], 0)


def attend_kernel(
    x01, x2, x3, seg0, seg1, seg2, seg3, bank, ag, ab,
    qs_ref, k_ref, v_ref, p_ref, o_ref, n1_ref, rs1_ref, bias,
):
    tokens_here, width = x2.shape
    batches = seg0.shape[0]
    length = tokens_here // batches
    qs_ref[...] = low(low(dot(x01[:tokens_here, :], of_bank(bank, 0))) * HEAD ** (-0.5))
    row = 0
    for piece in (x01, x2, x3):
        span = slice(row, row + piece.shape[0])
        k_ref[span, :] = low(dot(piece[...], of_bank(bank, 1)))
        v_ref[span, :] = low(dot(piece[...], of_bank(bank, 2)))
        row += piece.shape[0]
    segments = [ref[...].astype(F32) for ref in (seg0, seg1, seg2, seg3)]
    lane = lax.broadcasted_iota(jnp.int32, (1, 2 * HEAD), 1)
    first = (lane < HEAD).astype(BF)
    second = (lane >= HEAD).astype(BF)
    for batch in range(batches):
        query_seg = segments[0][batch : batch + 1, :]
        for index, segment in enumerate(segments):
            row = segment[batch : batch + 1, :]
            key_seg = jnp.transpose(jnp.broadcast_to(row, (length, length)))
            bias[pl.ds(index * length, length), :] = jnp.where(key_seg == query_seg, 0.0, -1e30)
        both = jnp.concatenate([bias[...], bias[...]], 1)
        for pair in range(width // (2 * HEAD)):
            lanes = slice(pair * 2 * HEAD, (pair + 1) * 2 * HEAD)
            kp = row_slices(k_ref, batch, length, lanes)
            vp = row_slices(v_ref, batch, length, lanes)
            qp = qs_ref[batch * length : (batch + 1) * length, lanes]
            stacked = jnp.concatenate([qp * first, qp * second], 0)
            scores = dot_nt(kp, stacked) + both
            exps = jnp.exp(scores - jnp.max(scores, 0, keepdims=True))
            probs = low(exps * (1.0 / jnp.sum(exps, 0, keepdims=True)))
            p_ref[batch * (width // (2 * HEAD)) + pair] = probs
            mixed = dot_tn(vp, probs)
            joined = jnp.concatenate([mixed[:HEAD, :length], mixed[HEAD:, length:]], 0)
            o_ref[batch * length : (batch + 1) * length, lanes] = low(jnp.transpose(joined))
    residual = x01[:tokens_here, :].astype(F32) + dot(o_ref[...], of_bank(bank, 3))
    _, unit, inv_std = normalize(residual, ag[...], ab[...])
    n1_ref[...] = unit
    rs1_ref[...] = jnp.broadcast_to(inv_std, rs1_ref.shape)


def feed_kernel(
    n1_ref, ag, ab, wi, bi, wu, mg, mb, bank, u_ref, sz_ref, n2_ref, rs2_ref, c_ref, st_ref
):
    width = n1_ref.shape[1]
    outer = n1_ref[...] * ag[...] + ab[...]
    al = low(outer)
    for part in range(wi.shape[1] // width):
        span = slice(part * width, (part + 1) * width)
        inner = dot(al, wi[:, span]) + bi[:, span]
        active, slope = gelu_both(inner)
        u_ref[:, span] = low(active)
        sz_ref[:, span] = low(slope)
        outer = outer + dot(low(active), wu[span, :])
    hidden, unit, inv_std = normalize(outer, mg[...], mb[...])
    n2_ref[...] = unit
    rs2_ref[...] = jnp.broadcast_to(inv_std, rs2_ref.shape)
    active, slope = gelu_both(dot(low(hidden), of_bank(bank, 4)))
    c_ref[...] = low(active)
    st_ref[...] = low(slope)


def joining_kernel(
    gathered, bottleneck, adapters, n2_ref, mg, mb, c_ref, st_ref, up, cot, fg, fb, *rest
):
    if gathered:
        jw_in, rest = rest[:8], rest[8:]
    else:
        jw_in, rest = rest[:1], rest[1:]
    out_ref, keep, send, dhp_ref, dt_ref, vec_ref, wj, left, right = rest
    width = n2_ref.shape[1]
    scale = width ** (-0.5)
    me = device_number()
    core = bit_of(me, 0)
    if gathered:
        shard, column = jw_in[0].shape[2:]
        for which in range(2):
            half = core if which == 0 else 1 - core
            columns = pl.ds(pl.multiple_of(half * column, column), column)
            for spot in range(8):
                flips = [sum(((spot >> i) & 1) << (order[i] - 2) for i in range(3)) for order in ORDER_JOIN]
                owner = jnp.bitwise_xor(lax.div(me, 4), jnp.where(half == 0, flips[0], flips[1]))
                rows = pl.ds(pl.multiple_of(owner * shard, shard), shard)
                for matrix in range(3):
                    wj[matrix, rows, columns] = jw_in[which * 4 + spot // 2][spot % 2, matrix]
    else:
        wj[...] = jw_in[0][...]
    hidden = n2_ref[...] * mg[...] + mb[...]
    hidden_low = low(hidden)
    cf = c_ref[...].astype(F32)
    row_group = lax.broadcasted_iota(jnp.int32, (width, 128), 0) // bottleneck
    column_of = lax.broadcasted_iota(jnp.int32, (width, 128), 1)
    member = (row_group == column_of).astype(BF)
    valid = lax.broadcasted_iota(jnp.int32, (1, 128), 1) < adapters

    def per_adapter(values):
        high = low(values)
        rest_of = low(values - high.astype(F32))
        return dot(high, member) + dot(rest_of, member)

    fq = low(dot(hidden_low, wj[0]))
    probe = low(dot_nt(fq, wj[1]))
    probe_f = probe.astype(F32)
    up_probe = dot_nt(probe, up[...])
    scores = (
        per_adapter(cf * up_probe) + jnp.sum(hidden * probe_f, -1, keepdims=True)
    ) * scale
    scores = jnp.where(valid, scores, -1e30)
    exps = jnp.exp(scores - jnp.max(scores, -1, keepdims=True))
    weights = exps * (1.0 / jnp.sum(exps, -1, keepdims=True))
    weights_low = low(weights)
    weights_wide = dot_nt(weights_low, member)
    weights_sum = jnp.sum(weights_low.astype(F32), -1, keepdims=True)
    mixed = low(weights_sum * hidden + dot(low(weights_wide * cf), up[...]))
    final, unit, inv_std = normalize(hidden + dot(mixed, wj[2]), fg[...], fb[...])
    out_ref[...] = low(final)
    d3, gain_term, shift_term = normalize_back(cot[...].astype(F32), unit, inv_std, fg[...])
    vec_ref[...] = jnp.concatenate(
        [gain_term, shift_term, jnp.zeros((vec_ref.shape[0] - 2, width), F32)], 0
    )
    dfo = low(d3)
    left[2] = mixed
    right[2] = dfo
    dm = low(dot_nt(dfo, wj[2]))
    dm_f = dm.astype(F32)
    up_dm = dot_nt(dm, up[...])
    dw = per_adapter(cf * up_dm) + jnp.sum(hidden * dm_f, -1, keepdims=True)
    df = low(weights * (dw - jnp.sum(weights * dw, -1, keepdims=True)))
    df_wide = dot_nt(df, member)
    df_sum = jnp.sum(df.astype(F32), -1, keepdims=True)
    dr = low((df_sum * hidden + dot(low(df_wide * cf), up[...])) * scale)
    left[1] = dr
    right[1] = fq
    dfq = low(dot(dr, wj[1]))
    left[0] = hidden_low
    right[0] = dfq
    for target, half, place in halves(keep, send, ORDERS["J"]):
        for matrix in range(3):
            term = low(dot_tn(half_columns(left.at[matrix], half), right[matrix]))
            put_blocks(target, term, matrix * (width // 2), place, 3 * width // GROUP)
    dc = weights_wide * up_dm + (df_wide * scale) * up_probe
    dt_ref[...] = low(dc * st_ref[...].astype(F32))
    dhp_ref[...] = (
        d3 + weights_sum * dm_f + (df_sum * scale) * probe_f + dot_nt(dfq, wj[0])
    )


def outer_back_kernel(
    dhp_ref, dt_ref, bank, n2_ref, rs2_ref, mg, u_ref, d2_ref, vec_ref, keep, send
):
    width = dhp_ref.shape[1]
    hidden_grad = dhp_ref[...] + dot_nt(dt_ref[...], of_bank(bank, 4))
    d2, mg_term, mb_term = normalize_back(hidden_grad, n2_ref[...], rs2_ref[:, :1], mg[...])
    d2_ref[...] = d2
    dfw = low(d2)
    units = u_ref.shape[1]
    for target, half, place in halves(keep, send, ORDERS["U"]):
        for begin in range(0, units // 2, width):
            term = low(dot_tn(half_columns(u_ref, half, begin, width), dfw))
            put_blocks(target, term, begin, place, units // GROUP)
    vec_ref[...] = jnp.concatenate([mg_term, mb_term, jnp.zeros((vec_ref.shape[0] - 2, width), F32)], 0)


def inner_back_kernel(
    d2_ref, sz_ref, wi, wu, n1_ref, rs1_ref, ag, ab, o_ref, vec_final, vec_middle,
    d1_ref, vec_ref, keep, send, dz_scr, dao_scr,
):
    width = d2_ref.shape[1]
    total = d2_ref[...]
    dfw = low(total)
    al = low(n1_ref[...] * ag[...] + ab[...])
    bias_terms = []
    parts = wi.shape[1] // width
    for part in range(parts):
        span = slice(part * width, (part + 1) * width)
        dz = low(dot_nt(dfw, wu[span, :]) * sz_ref[:, span].astype(F32))
        bias_terms.append(jnp.sum(dz.astype(F32), 0, keepdims=True))
        dz_scr[:, span] = dz
        total = total + dot_nt(dz, wi[:, span])
    d1, ag_term, ab_term = normalize_back(total, n1_ref[...], rs1_ref[:, :1], ag[...])
    d1_ref[...] = d1
    dao_scr[...] = low(d1)
    units = wi.shape[1]
    rows_each = (units + width) // GROUP
    for target, half, place in halves(keep, send, ORDERS["I"]):
        for begin in range(0, units // 2, width):
            term = low(dot_tn(al, half_columns(dz_scr, half, begin, width)))
            put_blocks(target, term, begin, place, rows_each)
        term = low(dot_tn(half_columns(o_ref, half), dao_scr[...]))
        put_blocks(target, term, units // 2, place, rows_each)
    rows = [ag_term, ab_term, vec_middle[0:1, :], vec_middle[1:2, :], vec_final[0:1, :], vec_final[1:2, :]]
    rows += bias_terms
    rows.append(jnp.zeros((vec_ref.shape[0] - len(rows), width), F32))
    vec_ref[...] = low(jnp.concatenate(rows, 0))


def attend_back_kernel(
    d1_ref, bank, o_ref, qs_ref, k_ref, v_ref, p_ref, x01, x2, x3, vec_ref,
    keep, send, dq_ref, dk_ref, dv_ref, do_scr, row_x,
):
    tokens_here, width = x2.shape
    length = p_ref.shape[2] // 2
    batches = tokens_here // length
    pairs = width // (2 * HEAD)
    do_scr[...] = low(dot_nt(low(d1_ref[...]), of_bank(bank, 3)))
    lane = lax.broadcasted_iota(jnp.int32, (1, 2 * HEAD), 1)
    first = (lane < HEAD).astype(BF)
    second = (lane >= HEAD).astype(BF)
    for batch in range(batches):
        here = slice(batch * length, (batch + 1) * length)
        spans = [
            slice(index * tokens_here + batch * length, index * tokens_here + (batch + 1) * length)
            for index in range(4)
        ]
        for pair in range(pairs):
            lanes = slice(pair * 2 * HEAD, (pair + 1) * 2 * HEAD)
            kp = row_slices(k_ref, batch, length, lanes)
            vp = row_slices(v_ref, batch, length, lanes)
            qp = qs_ref[here, lanes]
            dop = do_scr[here, lanes]
            q_stacked = jnp.concatenate([qp * first, qp * second], 0)
            do_stacked = jnp.concatenate([dop * first, dop * second], 0)
            probs = p_ref[batch * pairs + pair]
            op = o_ref[here, lanes].astype(F32)
            product = dop.astype(F32) * op
            high = low(product)
            rest = low(product - high.astype(F32))
            spread = jnp.concatenate([high * first, high * second], 0)
            spread_rest = jnp.concatenate([rest * first, rest * second], 0)
            ones = jnp.ones((8, 2 * HEAD), BF)
            shift = (dot_nt(ones, spread) + dot_nt(ones, spread_rest))[:1, :]
            ds = low(probs.astype(F32) * (dot_nt(vp, do_stacked) - shift))
            dv = low(dot(probs, do_stacked))
            dk = low(dot(ds, q_stacked))
            for index, span in enumerate(spans):
                rows = slice(index * length, (index + 1) * length)
                dk_ref[span, lanes] = dk[rows, :]
                dv_ref[span, lanes] = dv[rows, :]
            mixed = dot_tn(kp, ds)
            joined = jnp.concatenate([mixed[:HEAD, :length], mixed[HEAD:, length:]], 0)
            dq_ref[here, lanes] = low(jnp.transpose(joined) * HEAD ** (-0.5))
    row_x[: 2 * tokens_here, :] = x01[...]
    row_x[2 * tokens_here : 3 * tokens_here, :] = x2[...]
    row_x[3 * tokens_here :, :] = x3[...]
    rows_each = 3 * width // GROUP
    for target, half, place in halves(keep, send, ORDERS["T"]):
        terms = (
            dot_tn(half_columns(x01.at[:tokens_here, :], half), dq_ref[...]),
            dot_tn(half_columns(row_x, half), dk_ref[...]),
            dot_tn(half_columns(row_x, half), dv_ref[...]),
        )
        for matrix, term in enumerate(terms):
            put_blocks(target, low(term), matrix * (width // 2), place, rows_each)
        target[HALF * rows_each :, :] = vec_ref[...]


def input_back_kernel(d1_ref, dq_ref, dk_ref, dv_ref, bank, gi_own, gi_keep, gi_send):
    tokens_here = d1_ref.shape[0]
    parts = []
    for index in range(4):
        span = slice(index * tokens_here, (index + 1) * tokens_here)
        parts.append(dot_nt(dk_ref[span, :], of_bank(bank, 1)) + dot_nt(dv_ref[span, :], of_bank(bank, 2)))
    gi_own[...] = parts[0] + d1_ref[...] + dot_nt(dq_ref[...], of_bank(bank, 0))
    gi_keep[...] = low(parts[2])
    gi_send[:tokens_here, :] = low(parts[1])
    gi_send[tokens_here:, :] = low(parts[3])


def finish_kernel(orders, layout, whose, with_vec, parts, kept, *rest):
    sources, rest = rest[:parts], rest[parts:]
    if with_vec:
        vec, rest = rest[0], rest[1:]
    rest = rest[kept:]
    full, sems = rest[-2:]
    outs = rest[:-2]
    me = device_number()
    core = bit_of(me, 0)
    each = sources[0].shape[0] // (HALF // 2)
    half_rows = HALF * each
    width = full.shape[1]
    copies = []
    for number, which in enumerate(whose):
        lower, upper = sources[2 * number : 2 * number + 2]
        half = core if which == 0 else 1 - core
        place = own_place(me, orders, half)
        base = number * half_rows
        for spot in range(HALF):
            source = lower if spot < HALF // 2 else upper
            begin = (spot % (HALF // 2)) * each
            block = jnp.bitwise_xor(place, spot)
            full[pl.ds(pl.multiple_of(base + block * each, 8), each), :] = source[
                begin : begin + each, :
            ].astype(F32)
        row = base
        for out, pieces, by_column in layout:
            for piece in range(pieces):
                target = outs[out]
                if by_column:
                    size = target.shape[0]
                    column = pl.multiple_of((half * pieces + piece) * width, width)
                    target = target.at[:, pl.ds(column, width)]
                else:
                    size = target.shape[0] // 2
                    target = target.at[pl.ds(pl.multiple_of(half * size, size), size), :]
                source = full.at[pl.ds(row, size), :]
                copies.append(pltpu.make_async_copy(source, target, sems.at[len(copies)]))
                copies[-1].start()
                row += size
    if with_vec:
        values = vec[...].astype(F32)
        small = [out for out in outs if out.shape[0] == 1]
        for index in range(6):
            small[index][...] = values[index : index + 1, :]
        for part in range(small[6].shape[1] // width):
            small[6][:, part * width : (part + 1) * width] = values[6 + part : 7 + part, :]
    for copy in copies:
        copy.wait()


def call(kernel, name, microseconds, out_shapes, out_specs, in_specs, scratch, *operands, aliases=()):
    return pl.pallas_call(
        kernel,
        out_shape=out_shapes,
        in_specs=in_specs,
        out_specs=out_specs,
        scratch_shapes=scratch,
        input_output_aliases=dict(aliases),
        compiler_params=pltpu.CompilerParams(vmem_limit_bytes=32 * 1024 * 1024),
        cost_estimate=pl.CostEstimate(
            flops=int(microseconds * 1e4), bytes_accessed=int(microseconds * 1e2), transcendentals=0
        ),
        name=name,
    )(*operands)


def shape(dims, kind=BF):
    return jax.ShapeDtypeStruct(dims, kind)


def per_device(
    row_total,
    tokens, segments, cotangent, query_weight, key_weight, value_weight, out_weight,
    attend_gain, attend_bias, inner_weight, inner_bias, outer_weight, middle_gain, middle_bias,
    adapter_down, adapter_up, joining_query, joining_key, joining_value, final_gain, final_bias,
):
    batches, row_count, length, width = tokens.shape
    here = batches * row_count * length
    hidden_units = inner_weight.shape[1]
    adapters, bottleneck = adapter_up.shape[0], adapter_up.shape[1]
    devices = row_total * 4
    pairs = width // (2 * HEAD)

    def swap(values, partner):
        return lax.ppermute(values, AXES, [(d, partner(d)) for d in range(devices)])

    def over_bit(values, bit, label="over_bit"):
        with jax.named_scope(label):
            return swap(values, lambda d: d ^ (1 << bit))

    def over_stage(values, orders, stage, label="over_stage"):
        with jax.named_scope(label):
            return swap(values, lambda d: d ^ (1 << orders[d & 1][stage]))

    token = [lax.create_token()]

    def gate(values):
        return lax.optimization_barrier((token[0], values))[1]

    def mark(values):
        token[0], values = lax.optimization_barrier((token[0], values))
        return values

    row = lambda vector: vector.reshape(1, -1)

    gathered = row_total == 8 and joining_query.shape[0] % 16 == 0
    stacked = jnp.stack([joining_query, joining_key, joining_value], 0)
    if gathered:
        core = lax.rem(lax.axis_index("tok"), 2)
        column = width // 2
        piece = lax.dynamic_slice_in_dim(stacked, core * column, column, 2)[None]
        far = over_stage(piece, ORDER_JOIN, 0, "weights_first")

    x0 = tokens.reshape(here, width)
    x2 = over_bit(x0, 1, "row_far")
    x1 = over_bit(x0, 0, "row_near")
    seg = segments.reshape(batches, length)
    with jax.named_scope("segments"):
        segs = [seg] + [swap(seg, lambda d, flip=flip: d ^ flip) for flip in (1, 2, 3)]
    if gathered:
        far = mark(far)
    if gathered:
        near = mark(jnp.concatenate([piece, gate(far)], 0))
        far = over_stage(near, ORDER_JOIN, 1, "weights_second")
    bank = mark(
        jnp.concatenate([gate(query_weight), key_weight, value_weight, out_weight, adapter_down], 1)
    )
    x01 = mark(jnp.concatenate([x0, gate(x1)], 0))
    segs = mark(segs)
    x2 = mark(x2)
    x3 = over_bit(x2, 0, "row_cross")
    if gathered:
        far = mark(far)
        third = [over_stage(part, ORDER_JOIN, 2, "weights_third") for part in (near, far)]
    else:
        jw = (lax.all_gather(stacked, "rows", axis=1, tiled=True),)

    x3 = mark(x3)
    qs, keys, values, probs, attended, n1, rs1 = call(
        attend_kernel,
        "attend",
        6,
        (
            shape((here, width)), shape((4 * here, width)), shape((4 * here, width)),
            shape((batches * pairs, 4 * length, 2 * length)), shape((here, width)),
            shape((here, width), F32), shape((here, 128), F32),
        ),
        (VM,) * 7,
        (VM,) * 10,
        [pltpu.VMEM((4 * length, length), F32)],
        x01, x2, x3, *segs, bank,
        gate(row(attend_gain)), row(attend_bias),
    )
    if gathered:
        n1 = mark(n1)
        third = mark(third)
        jw = (near, far, *third)
        jw += tuple(over_bit(gate(part), 0, "weights_core") for part in jw)
    active, slope_z, n2, rs2, bottle, slope_t = call(
        feed_kernel,
        "feed",
        3,
        (
            shape((here, hidden_units)), shape((here, hidden_units)), shape((here, width), F32),
            shape((here, 128), F32), shape((here, width)), shape((here, width)),
        ),
        (VM,) * 6,
        (VM,) * 9,
        [],
        n1, row(attend_gain), row(attend_bias), inner_weight, row(inner_bias), outer_weight,
        gate(row(middle_gain)), row(middle_bias), bank,
    )
    n2 = mark(n2)

    waiting = []

    def later(values, travel, put):
        waiting.append((values, travel, put, len(waiting)))

    def start_waiting():
        for values, travel, put, place in waiting:
            put(travel(values if place == len(waiting) - 1 else gate(values)))
        waiting.clear()

    class Stream:
        def __init__(self, name, orders, rows_each):
            self.name, self.orders, self.rows_each, self.count = name, orders, rows_each, 0

        def send(self, values, stage, label, into="got"):
            def travel(operand):
                with jax.named_scope(f"{self.name}_{label}"):
                    if stage is None:
                        return over_bit(operand, 0)
                    return over_stage(operand, self.orders, stage)

            later(values, travel, lambda result: setattr(self, into, result))

        def begin(self, keep, send):
            self.keep, self.rows = keep, HALF * self.rows_each
            self.send(mark(send), None, "core")

        def step(self):
            stage, self.count = self.count, self.count + 1
            label = f"step_{stage}"
            keep, got = self.keep, gate(self.got)
            if stage < 4:
                middle = self.rows // 2
                send = mark(keep[middle:] + got[middle:])
                self.send(send, stage, label)
                self.keep = jnp.concatenate(
                    [keep[:middle] + got[:middle], keep[self.rows :] + got[self.rows :]], 0
                )
                self.rows = middle
            elif stage == 4:
                block = keep + got
                for bit in range(5, devices.bit_length() - 1):
                    block = block + over_bit(block, bit)
                self.extra = block[self.rows_each :]
                self.keep = mark(block[: self.rows_each])
                self.send(self.keep, 3, label)
            elif stage < 8:
                self.keep = mark(jnp.concatenate([keep, got], 0))
                self.send(self.keep, 7 - stage, label)
                if stage == 7:
                    self.send(self.keep, None, "sibling", "sibling")
            else:
                self.got, self.sibling = mark((got, self.sibling))
                self.send(self.got, None, "upper", "upper")

        def parts(self):
            return self.keep, self.got, self.sibling, getattr(self, "upper", None)

    def finish(stream, outs, layout, name, vector=None, whose=(0, 1), kept=()):
        sources = stream.parts()[2 * whose[0] : 2 * whose[-1] + 2]
        sources = list(sources[:-1]) + [gate(sources[-1])]
        vectors = [] if vector is None else [vector]
        small = [] if vector is None else [shape((1, width), F32)] * 6 + [shape((1, hidden_units), F32)]
        rows = sources[0].shape[0] * 2 * len(whose)
        first = len(sources) + len(vectors)
        out = call(
            functools.partial(
                finish_kernel, stream.orders, layout, whose, vector is not None, len(sources), len(kept)
            ),
            name,
            2,
            tuple(outs) + tuple(small),
            (ANY,) * len(outs) + (VM,) * len(small),
            (VM,) * first + (ANY,) * len(kept),
            [pltpu.VMEM((rows, width), F32), pltpu.SemaphoreType.DMA((8,))],
            *sources, *vectors, *kept,
            aliases=[(first + index, index) for index in range(len(kept))],
        )
        out = list(out)
        out[0] = mark(out[0])
        return out

    blocks = hidden_units // width
    square = shape((width, width), F32)
    each = lambda count: count * width // GROUP
    streams = {
        "J": Stream("joining_sum", ORDERS["J"], each(3)),
        "U": Stream("outer_sum", ORDERS["U"], each(blocks)),
        "I": Stream("inner_sum", ORDERS["I"], each(blocks + 1)),
        "T": Stream("attend_sum", ORDERS["T"], each(3)),
    }
    done = {}

    half_rows = lambda count: count * width // 2
    up = adapter_up.reshape(adapters * bottleneck, width)

    def joining_step():
        done["output"], keep, send, done["dhp"], done["dt"], done["vec_final"] = call(
            functools.partial(joining_kernel, gathered, bottleneck, adapters),
            "joining",
            8,
            (
                shape((here, width)), shape((half_rows(3), width)), shape((half_rows(3), width)),
                shape((here, width), F32), shape((here, width)), shape((8, width), F32),
            ),
            (VM,) * 6,
            (VM,) * (9 + len(jw)),
            [
                pltpu.VMEM((3, width, width), BF), pltpu.VMEM((3, here, width), BF),
                pltpu.VMEM((3, here, width), BF),
            ],
            n2, row(middle_gain), row(middle_bias), bottle, slope_t, up, cotangent.reshape(here, width),
            row(final_gain), row(final_bias), *jw,
        )
        streams["J"].begin(keep, send)

    def outer_step():
        done["d2"], done["vec_middle"], keep, send = call(
            outer_back_kernel,
            "outer_back",
            4,
            (
                shape((here, width), F32), shape((8, width), F32),
                shape((half_rows(blocks), width)), shape((half_rows(blocks), width)),
            ),
            (VM,) * 4,
            (VM,) * 7,
            [],
            done["dhp"], done["dt"], bank, n2, rs2, gate(row(middle_gain)), active,
        )
        streams["U"].begin(keep, send)

    def inner_step():
        done["d1"], done["vec"], keep, send = call(
            inner_back_kernel,
            "inner_back",
            6,
            (
                shape((here, width), F32), shape((16, width)),
                shape((half_rows(blocks + 1), width)), shape((half_rows(blocks + 1), width)),
            ),
            (VM,) * 4,
            (VM,) * 11,
            [pltpu.VMEM((here, hidden_units), BF), pltpu.VMEM((here, width), BF)],
            done["d2"], slope_z, inner_weight, outer_weight, n1, rs1, gate(row(attend_gain)),
            row(attend_bias), attended, done["vec_final"], done["vec_middle"],
        )
        streams["I"].begin(keep, send)

    def attend_step():
        keep, send, done["dq"], done["dk"], done["dv"] = call(
            attend_back_kernel,
            "attend_back",
            8,
            (
                shape((half_rows(3) + 16, width)), shape((half_rows(3) + 16, width)),
                shape((here, width)), shape((4 * here, width)), shape((4 * here, width)),
            ),
            (VM,) * 5,
            (VM,) * 11,
            [pltpu.VMEM((here, width), BF), pltpu.VMEM((4 * here, width), BF)],
            done["d1"], bank, attended, qs, keys, values, probs, x01, x2, x3, gate(done["vec"]),
        )
        streams["T"].begin(keep, send)

    def input_step():
        own, keep, send = call(
            input_back_kernel,
            "input_back",
            2,
            (shape((here, width), F32), shape((here, width)), shape((2 * here, width))),
            (VM,) * 3,
            (VM,) * 5,
            [],
            gate(done["d1"]), done["dq"], done["dk"], done["dv"], bank,
        )
        keep = mark(keep)
        done["gi"] = (own, keep)
        later(send, lambda values: over_bit(values, 0), lambda result: done.update(near=result))

    kernels = {"KJ": joining_step, "KU": outer_step, "KI": inner_step, "KT": attend_step, "KG": input_step}

    def run(plan):
        for step in [step for group in plan for step in group + (None,)]:
            if step is None:
                start_waiting()
            elif step in kernels:
                kernels[step]()
            elif step == "fJ":
                done["J"] = finish(streams["J"], [square] * 3, THREE, "finish_joining")
            elif step == "fU":
                done["U"] = finish(
                    streams["U"], [shape((hidden_units, width), F32)], ((0, 1, False),), "finish_outer"
                )
            elif step == "fI":
                done["I"] = finish(
                    streams["I"], [shape((width, hidden_units), F32), square],
                    ((0, blocks // 2, True), (1, 1, False)), "finish_inner",
                )
            elif step == "fT":
                done["T"] = finish(
                    streams["T"], [square] * 3, THREE, "finish_attend", streams["T"].extra, (1,), done["hT"]
                )
            elif step == "hT":
                done["hT"] = finish(streams["T"], [square] * 3, THREE, "finish_half", whose=(0,))
            elif step == "g0":
                got = gate(done["near"])
                send = mark(done["gi"][1] + got[here:])
                later(send, lambda values: over_bit(values, 1), lambda result: done.update(far=result))
                done["near"] = got[:here]
            elif step == "g1":
                far = gate(done["far"])
                done["input"] = mark(low(done["gi"][0] + done["near"].astype(F32) + far.astype(F32)))
            else:
                streams[step].step()

    run(PLAN)
    last, inner, out_grad = done["T"], done["I"][0], done["I"][1]
    outer, joining, output, input_grad = done["U"][0], done["J"], done["output"], done["input"]
    flat = lambda values: values.reshape(-1)
    return (
        output.reshape(tokens.shape), input_grad.reshape(tokens.shape),
        last[0], last[1], last[2], out_grad, flat(last[3]), flat(last[4]),
        inner, flat(last[9]), outer, flat(last[5]), flat(last[6]),
        joining[0], joining[1], joining[2], flat(last[7]), flat(last[8]),
    )


def solution(mesh):
    return jax.shard_map(
        functools.partial(per_device, mesh.shape["rows"]),
        mesh=mesh,
        in_specs=(
            P(None, "rows", "tok", None), P(None, "rows", "tok"), P(None, "rows", "tok", None),
        ) + (P(),) * 13 + (P("rows", None),) * 3 + (P(),) * 2,
        out_specs=(P(None, "rows", "tok", None),) * 2 + (P(),) * 16,
        check_vma=False,
    )
```

```python
import functools

import jax
import jax.numpy as jnp
from jax import lax
from jax.experimental import pallas as pl
from jax.experimental.pallas import tpu as pltpu
from jax.sharding import PartitionSpec as P

HEAD = 64
AXES = ("rows", "tok")
BF = jnp.bfloat16
F32 = jnp.float32
norm_eps = 1e-06

ORDER_XY = ((1, 2, 3, 4), (2, 1, 3, 4))
ORDER_YX = ((2, 1, 3, 4), (1, 2, 3, 4))
ORDER_Z = ((3, 4, 1, 2), (4, 3, 2, 1))
ORDER_ZY = ((4, 3, 1, 2), (3, 4, 2, 1))
ORDERS = {"J": ORDER_XY, "U": ORDER_Z, "I": ORDER_XY, "T": ORDER_XY}
ORDER_JOIN = ((2, 4, 3), (4, 3, 2))
GROUP = 32
THREE = ((0, 1, False), (1, 1, False), (2, 1, False))
PLAN = (
    ("KJ",), ("KU",), ("KI",), ("J", "U",), ("I",), ("KT",), ("KG", "J", "U", "I", "T",), ("I", "U",),
    ("T",), ("I", "J", "g0", "U", "T",), ("I",), ("U", "J",), ("I",), ("U", "T", "J",), ("J",),
    ("I", "U", "T",), ("g1",), ("J",), ("T",), ("I", "J", "U",), ("I", "T",), ("J", "T",), ("U",),
    ("fI", "fJ", "fU",), ("T",), ("hT",), ("fT",),
)
HALF = GROUP // 2

VM = pl.BlockSpec(memory_space=pltpu.VMEM)
ANY = pl.BlockSpec(memory_space=pl.ANY)


def dot(left, right):
    return jnp.dot(left, right, preferred_element_type=F32)


def dot_tn(left, right):
    return lax.dot_general(left, right, (((0,), (0,)), ((), ())), preferred_element_type=F32)


def dot_nt(left, right):
    return lax.dot_general(left, right, (((1,), (1,)), ((), ())), preferred_element_type=F32)


def low(values):
    return values.astype(BF)


def normalize(values, gain, shift):
    centered = values - jnp.mean(values, -1, keepdims=True)
    inv_std = lax.rsqrt(jnp.mean(centered * centered, -1, keepdims=True) + norm_eps)
    unit = centered * inv_std
    return unit * gain + shift, unit, inv_std


def normalize_back(upstream, unit, inv_std, gain):
    grad_unit = upstream * gain
    projected = grad_unit - jnp.mean(grad_unit, -1, keepdims=True)
    projected = projected - unit * jnp.mean(grad_unit * unit, -1, keepdims=True)
    gain_term = jnp.sum(upstream * unit, 0, keepdims=True)
    return projected * inv_std, gain_term, jnp.sum(upstream, 0, keepdims=True)


def gelu_both(values):
    normal_cdf = 0.5 * (1.0 + lax.erf(values * 0.7071067811865476))
    slope = normal_cdf + values * jnp.exp(-0.5 * values * values) * 0.3989422804014327
    return values * normal_cdf, slope


def device_number():
    return lax.axis_index("rows") * 4 + lax.axis_index("tok")


def bit_of(number, bit):
    return lax.rem(lax.div(number, 1 << bit), 2)


def own_place(number, orders, core):
    def along(order):
        total = 0
        for bit in order:
            total = total * 2 + bit_of(number, bit)
        return total

    return jnp.where(core == 0, along(orders[0]), along(orders[1]))


def put_blocks(target, values, first_row, place, rows_each):
    row = first_row
    while row < first_row + values.shape[0]:
        block, within = divmod(row, rows_each)
        count = min(rows_each - within, first_row + values.shape[0] - row)
        spot = jnp.bitwise_xor(place, block) * rows_each + within
        target[pl.ds(pl.multiple_of(spot, 16), count), :] = values[row - first_row : row - first_row + count, :]
        row += count


def halves(keep, send, orders):
    me = device_number()
    core = bit_of(me, 0)
    return (
        (keep, core, own_place(me, orders, core)),
        (send, 1 - core, own_place(me, orders, 1 - core)),
    )


def half_columns(ref, half, begin=0, count=None):
    size = ref.shape[1] // 2
    count = size if count is None else count
    return ref[:, pl.ds(pl.multiple_of(half * size + begin, 128), count)]


def of_bank(bank, index):
    width = bank.shape[0]
    return bank[:, index * width : (index + 1) * width]


def row_slices(ref, batch, length, lanes):
    here = ref.shape[0] // 4
    begins = [place * here + batch * length for place in range(4)]
    return jnp.concatenate([ref[begin : begin + length, lanes] for begin in begins], 0)


def attend_kernel(
    x01, x2, x3, seg0, seg1, seg2, seg3, bank, ag, ab,
    qs_ref, k_ref, v_ref, p_ref, o_ref, n1_ref, rs1_ref, bias,
):
    tokens_here, width = x2.shape
    batches = seg0.shape[0]
    length = tokens_here // batches
    qs_ref[...] = low(low(dot(x01[:tokens_here, :], of_bank(bank, 0))) * HEAD ** (-0.5))
    row = 0
    for piece in (x01, x2, x3):
        span = slice(row, row + piece.shape[0])
        k_ref[span, :] = low(dot(piece[...], of_bank(bank, 1)))
        v_ref[span, :] = low(dot(piece[...], of_bank(bank, 2)))
        row += piece.shape[0]
    segments = [ref[...].astype(F32) for ref in (seg0, seg1, seg2, seg3)]
    lane = lax.broadcasted_iota(jnp.int32, (1, 2 * HEAD), 1)
    first = (lane < HEAD).astype(BF)
    second = (lane >= HEAD).astype(BF)
    for batch in range(batches):
        query_seg = segments[0][batch : batch + 1, :]
        for index, segment in enumerate(segments):
            row = segment[batch : batch + 1, :]
            key_seg = jnp.transpose(jnp.broadcast_to(row, (length, length)))
            bias[pl.ds(index * length, length), :] = jnp.where(key_seg == query_seg, 0.0, -1e30)
        both = jnp.concatenate([bias[...], bias[...]], 1)
        for pair in range(width // (2 * HEAD)):
            lanes = slice(pair * 2 * HEAD, (pair + 1) * 2 * HEAD)
            kp = row_slices(k_ref, batch, length, lanes)
            vp = row_slices(v_ref, batch, length, lanes)
            qp = qs_ref[batch * length : (batch + 1) * length, lanes]
            stacked = jnp.concatenate([qp * first, qp * second], 0)
            scores = dot_nt(kp, stacked) + both
            exps = jnp.exp(scores - jnp.max(scores, 0, keepdims=True))
            probs = low(exps * (1.0 / jnp.sum(exps, 0, keepdims=True)))
            p_ref[batch * (width // (2 * HEAD)) + pair] = probs
            mixed = dot_tn(vp, probs)
            joined = jnp.concatenate([mixed[:HEAD, :length], mixed[HEAD:, length:]], 0)
            o_ref[batch * length : (batch + 1) * length, lanes] = low(jnp.transpose(joined))
    residual = x01[:tokens_here, :].astype(F32) + dot(o_ref[...], of_bank(bank, 3))
    _, unit, inv_std = normalize(residual, ag[...], ab[...])
    n1_ref[...] = unit
    rs1_ref[...] = jnp.broadcast_to(inv_std, rs1_ref.shape)


def feed_kernel(
    n1_ref, ag, ab, wi, bi, wu, mg, mb, bank, u_ref, sz_ref, n2_ref, rs2_ref, c_ref, st_ref
):
    width = n1_ref.shape[1]
    outer = n1_ref[...] * ag[...] + ab[...]
    al = low(outer)
    for part in range(wi.shape[1] // width):
        span = slice(part * width, (part + 1) * width)
        inner = dot(al, wi[:, span]) + bi[:, span]
        active, slope = gelu_both(inner)
        u_ref[:, span] = low(active)
        sz_ref[:, span] = low(slope)
        outer = outer + dot(low(active), wu[span, :])
    hidden, unit, inv_std = normalize(outer, mg[...], mb[...])
    n2_ref[...] = unit
    rs2_ref[...] = jnp.broadcast_to(inv_std, rs2_ref.shape)
    active, slope = gelu_both(dot(low(hidden), of_bank(bank, 4)))
    c_ref[...] = low(active)
    st_ref[...] = low(slope)


def joining_kernel(
    gathered, bottleneck, adapters, n2_ref, mg, mb, c_ref, st_ref, up, cot, fg, fb, *rest
):
    if gathered:
        jw_in, rest = rest[:8], rest[8:]
    else:
        jw_in, rest = rest[:1], rest[1:]
    out_ref, keep, send, dhp_ref, dt_ref, vec_ref, wj, left, right = rest
    width = n2_ref.shape[1]
    scale = width ** (-0.5)
    me = device_number()
    core = bit_of(me, 0)
    if gathered:
        shard, column = jw_in[0].shape[2:]
        for which in range(2):
            half = core if which == 0 else 1 - core
            columns = pl.ds(pl.multiple_of(half * column, column), column)
            for spot in range(8):
                flips = [sum(((spot >> i) & 1) << (order[i] - 2) for i in range(3)) for order in ORDER_JOIN]
                owner = jnp.bitwise_xor(lax.div(me, 4), jnp.where(half == 0, flips[0], flips[1]))
                rows = pl.ds(pl.multiple_of(owner * shard, shard), shard)
                for matrix in range(3):
                    wj[matrix, rows, columns] = jw_in[which * 4 + spot // 2][spot % 2, matrix]
    else:
        wj[...] = jw_in[0][...]
    hidden = n2_ref[...] * mg[...] + mb[...]
    hidden_low = low(hidden)
    cf = c_ref[...].astype(F32)
    row_group = lax.broadcasted_iota(jnp.int32, (width, 128), 0) // bottleneck
    column_of = lax.broadcasted_iota(jnp.int32, (width, 128), 1)
    member = (row_group == column_of).astype(BF)
    valid = lax.broadcasted_iota(jnp.int32, (1, 128), 1) < adapters

    def per_adapter(values):
        high = low(values)
        rest_of = low(values - high.astype(F32))
        return dot(high, member) + dot(rest_of, member)

    fq = low(dot(hidden_low, wj[0]))
    probe = low(dot_nt(fq, wj[1]))
    probe_f = probe.astype(F32)
    up_probe = dot_nt(probe, up[...])
    scores = (
        per_adapter(cf * up_probe) + jnp.sum(hidden * probe_f, -1, keepdims=True)
    ) * scale
    scores = jnp.where(valid, scores, -1e30)
    exps = jnp.exp(scores - jnp.max(scores, -1, keepdims=True))
    weights = exps * (1.0 / jnp.sum(exps, -1, keepdims=True))
    weights_low = low(weights)
    weights_wide = dot_nt(weights_low, member)
    weights_sum = jnp.sum(weights_low.astype(F32), -1, keepdims=True)
    mixed = low(weights_sum * hidden + dot(low(weights_wide * cf), up[...]))
    final, unit, inv_std = normalize(hidden + dot(mixed, wj[2]), fg[...], fb[...])
    out_ref[...] = low(final)
    d3, gain_term, shift_term = normalize_back(cot[...].astype(F32), unit, inv_std, fg[...])
    vec_ref[...] = jnp.concatenate(
        [gain_term, shift_term, jnp.zeros((vec_ref.shape[0] - 2, width), F32)], 0
    )
    dfo = low(d3)
    left[2] = mixed
    right[2] = dfo
    dm = low(dot_nt(dfo, wj[2]))
    dm_f = dm.astype(F32)
    up_dm = dot_nt(dm, up[...])
    dw = per_adapter(cf * up_dm) + jnp.sum(hidden * dm_f, -1, keepdims=True)
    df = low(weights * (dw - jnp.sum(weights * dw, -1, keepdims=True)))
    df_wide = dot_nt(df, member)
    df_sum = jnp.sum(df.astype(F32), -1, keepdims=True)
    dr = low((df_sum * hidden + dot(low(df_wide * cf), up[...])) * scale)
    left[1] = dr
    right[1] = fq
    dfq = low(dot(dr, wj[1]))
    left[0] = hidden_low
    right[0] = dfq
    for target, half, place in halves(keep, send, ORDERS["J"]):
        for matrix in range(3):
            term = low(dot_tn(half_columns(left.at[matrix], half), right[matrix]))
            put_blocks(target, term, matrix * (width // 2), place, 3 * width // GROUP)
    dc = weights_wide * up_dm + (df_wide * scale) * up_probe
    dt_ref[...] = low(dc * st_ref[...].astype(F32))
    dhp_ref[...] = (
        d3 + weights_sum * dm_f + (df_sum * scale) * probe_f + dot_nt(dfq, wj[0])
    )


def outer_back_kernel(
    dhp_ref, dt_ref, bank, n2_ref, rs2_ref, mg, u_ref, d2_ref, vec_ref, keep, send
):
    width = dhp_ref.shape[1]
    hidden_grad = dhp_ref[...] + dot_nt(dt_ref[...], of_bank(bank, 4))
    d2, mg_term, mb_term = normalize_back(hidden_grad, n2_ref[...], rs2_ref[:, :1], mg[...])
    d2_ref[...] = d2
    dfw = low(d2)
    units = u_ref.shape[1]
    for target, half, place in halves(keep, send, ORDERS["U"]):
        for begin in range(0, units // 2, width):
            term = low(dot_tn(half_columns(u_ref, half, begin, width), dfw))
            put_blocks(target, term, begin, place, units // GROUP)
    vec_ref[...] = jnp.concatenate([mg_term, mb_term, jnp.zeros((vec_ref.shape[0] - 2, width), F32)], 0)


def inner_back_kernel(
    d2_ref, sz_ref, wi, wu, n1_ref, rs1_ref, ag, ab, o_ref, vec_final, vec_middle,
    d1_ref, vec_ref, keep, send, dz_scr, dao_scr,
):
    width = d2_ref.shape[1]
    total = d2_ref[...]
    dfw = low(total)
    al = low(n1_ref[...] * ag[...] + ab[...])
    bias_terms = []
    parts = wi.shape[1] // width
    for part in range(parts):
        span = slice(part * width, (part + 1) * width)
        dz = low(dot_nt(dfw, wu[span, :]) * sz_ref[:, span].astype(F32))
        bias_terms.append(jnp.sum(dz.astype(F32), 0, keepdims=True))
        dz_scr[:, span] = dz
        total = total + dot_nt(dz, wi[:, span])
    d1, ag_term, ab_term = normalize_back(total, n1_ref[...], rs1_ref[:, :1], ag[...])
    d1_ref[...] = d1
    dao_scr[...] = low(d1)
    units = wi.shape[1]
    rows_each = (units + width) // GROUP
    for target, half, place in halves(keep, send, ORDERS["I"]):
        for begin in range(0, units // 2, width):
            term = low(dot_tn(al, half_columns(dz_scr, half, begin, width)))
            put_blocks(target, term, begin, place, rows_each)
        term = low(dot_tn(half_columns(o_ref, half), dao_scr[...]))
        put_blocks(target, term, units // 2, place, rows_each)
    rows = [ag_term, ab_term, vec_middle[0:1, :], vec_middle[1:2, :], vec_final[0:1, :], vec_final[1:2, :]]
    rows += bias_terms
    rows.append(jnp.zeros((vec_ref.shape[0] - len(rows), width), F32))
    vec_ref[...] = low(jnp.concatenate(rows, 0))


def attend_back_kernel(
    d1_ref, bank, o_ref, qs_ref, k_ref, v_ref, p_ref, x01, x2, x3, vec_ref,
    keep, send, dq_ref, dk_ref, dv_ref, do_scr, row_x,
):
    tokens_here, width = x2.shape
    length = p_ref.shape[2] // 2
    batches = tokens_here // length
    pairs = width // (2 * HEAD)
    do_scr[...] = low(dot_nt(low(d1_ref[...]), of_bank(bank, 3)))
    lane = lax.broadcasted_iota(jnp.int32, (1, 2 * HEAD), 1)
    first = (lane < HEAD).astype(BF)
    second = (lane >= HEAD).astype(BF)
    for batch in range(batches):
        here = slice(batch * length, (batch + 1) * length)
        spans = [
            slice(index * tokens_here + batch * length, index * tokens_here + (batch + 1) * length)
            for index in range(4)
        ]
        for pair in range(pairs):
            lanes = slice(pair * 2 * HEAD, (pair + 1) * 2 * HEAD)
            kp = row_slices(k_ref, batch, length, lanes)
            vp = row_slices(v_ref, batch, length, lanes)
            qp = qs_ref[here, lanes]
            dop = do_scr[here, lanes]
            q_stacked = jnp.concatenate([qp * first, qp * second], 0)
            do_stacked = jnp.concatenate([dop * first, dop * second], 0)
            probs = p_ref[batch * pairs + pair]
            op = o_ref[here, lanes].astype(F32)
            product = dop.astype(F32) * op
            high = low(product)
            rest = low(product - high.astype(F32))
            spread = jnp.concatenate([high * first, high * second], 0)
            spread_rest = jnp.concatenate([rest * first, rest * second], 0)
            ones = jnp.ones((8, 2 * HEAD), BF)
            shift = (dot_nt(ones, spread) + dot_nt(ones, spread_rest))[:1, :]
            ds = low(probs.astype(F32) * (dot_nt(vp, do_stacked) - shift))
            dv = low(dot(probs, do_stacked))
            dk = low(dot(ds, q_stacked))
            for index, span in enumerate(spans):
                rows = slice(index * length, (index + 1) * length)
                dk_ref[span, lanes] = dk[rows, :]
                dv_ref[span, lanes] = dv[rows, :]
            mixed = dot_tn(kp, ds)
            joined = jnp.concatenate([mixed[:HEAD, :length], mixed[HEAD:, length:]], 0)
            dq_ref[here, lanes] = low(jnp.transpose(joined) * HEAD ** (-0.5))
    row_x[: 2 * tokens_here, :] = x01[...]
    row_x[2 * tokens_here : 3 * tokens_here, :] = x2[...]
    row_x[3 * tokens_here :, :] = x3[...]
    rows_each = 3 * width // GROUP
    for target, half, place in halves(keep, send, ORDERS["T"]):
        terms = (
            dot_tn(half_columns(x01.at[:tokens_here, :], half), dq_ref[...]),
            dot_tn(half_columns(row_x, half), dk_ref[...]),
            dot_tn(half_columns(row_x, half), dv_ref[...]),
        )
        for matrix, term in enumerate(terms):
            put_blocks(target, low(term), matrix * (width // 2), place, rows_each)
        target[HALF * rows_each :, :] = vec_ref[...]


def input_back_kernel(d1_ref, dq_ref, dk_ref, dv_ref, bank, gi_own, gi_keep, gi_send):
    tokens_here = d1_ref.shape[0]
    parts = []
    for index in range(4):
        span = slice(index * tokens_here, (index + 1) * tokens_here)
        parts.append(dot_nt(dk_ref[span, :], of_bank(bank, 1)) + dot_nt(dv_ref[span, :], of_bank(bank, 2)))
    gi_own[...] = parts[0] + d1_ref[...] + dot_nt(dq_ref[...], of_bank(bank, 0))
    gi_keep[...] = low(parts[2])
    gi_send[:tokens_here, :] = low(parts[1])
    gi_send[tokens_here:, :] = low(parts[3])


def finish_kernel(orders, layout, whose, with_vec, parts, kept, *rest):
    sources, rest = rest[:parts], rest[parts:]
    if with_vec:
        vec, rest = rest[0], rest[1:]
    rest = rest[kept:]
    full, sems = rest[-2:]
    outs = rest[:-2]
    me = device_number()
    core = bit_of(me, 0)
    each = sources[0].shape[0] // (HALF // 2)
    half_rows = HALF * each
    width = full.shape[1]
    copies = []
    for number, which in enumerate(whose):
        lower, upper = sources[2 * number : 2 * number + 2]
        half = core if which == 0 else 1 - core
        place = own_place(me, orders, half)
        base = number * half_rows
        for spot in range(HALF):
            source = lower if spot < HALF // 2 else upper
            begin = (spot % (HALF // 2)) * each
            block = jnp.bitwise_xor(place, spot)
            full[pl.ds(pl.multiple_of(base + block * each, 8), each), :] = source[
                begin : begin + each, :
            ].astype(F32)
        row = base
        for out, pieces, by_column in layout:
            for piece in range(pieces):
                target = outs[out]
                if by_column:
                    size = target.shape[0]
                    column = pl.multiple_of((half * pieces + piece) * width, width)
                    target = target.at[:, pl.ds(column, width)]
                else:
                    size = target.shape[0] // 2
                    target = target.at[pl.ds(pl.multiple_of(half * size, size), size), :]
                source = full.at[pl.ds(row, size), :]
                copies.append(pltpu.make_async_copy(source, target, sems.at[len(copies)]))
                copies[-1].start()
                row += size
    if with_vec:
        values = vec[...].astype(F32)
        small = [out for out in outs if out.shape[0] == 1]
        for index in range(6):
            small[index][...] = values[index : index + 1, :]
        for part in range(small[6].shape[1] // width):
            small[6][:, part * width : (part + 1) * width] = values[6 + part : 7 + part, :]
    for copy in copies:
        copy.wait()


def call(kernel, name, microseconds, out_shapes, out_specs, in_specs, scratch, *operands, aliases=()):
    return pl.pallas_call(
        kernel,
        out_shape=out_shapes,
        in_specs=in_specs,
        out_specs=out_specs,
        scratch_shapes=scratch,
        input_output_aliases=dict(aliases),
        compiler_params=pltpu.CompilerParams(vmem_limit_bytes=32 * 1024 * 1024),
        cost_estimate=pl.CostEstimate(
            flops=int(microseconds * 1e4), bytes_accessed=int(microseconds * 1e2), transcendentals=0
        ),
        name=name,
    )(*operands)


def shape(dims, kind=BF):
    return jax.ShapeDtypeStruct(dims, kind)


def per_device(
    row_total,
    tokens, segments, cotangent, query_weight, key_weight, value_weight, out_weight,
    attend_gain, attend_bias, inner_weight, inner_bias, outer_weight, middle_gain, middle_bias,
    adapter_down, adapter_up, joining_query, joining_key, joining_value, final_gain, final_bias,
):
    batches, row_count, length, width = tokens.shape
    here = batches * row_count * length
    hidden_units = inner_weight.shape[1]
    adapters, bottleneck = adapter_up.shape[0], adapter_up.shape[1]
    devices = row_total * 4
    pairs = width // (2 * HEAD)

    def swap(values, partner):
        return lax.ppermute(values, AXES, [(d, partner(d)) for d in range(devices)])

    def over_bit(values, bit, label="over_bit"):
        with jax.named_scope(label):
            return swap(values, lambda d: d ^ (1 << bit))

    def over_stage(values, orders, stage, label="over_stage"):
        with jax.named_scope(label):
            return swap(values, lambda d: d ^ (1 << orders[d & 1][stage]))

    token = [lax.create_token()]

    def gate(values):
        return lax.optimization_barrier((token[0], values))[1]

    def mark(values):
        token[0], values = lax.optimization_barrier((token[0], values))
        return values

    row = lambda vector: vector.reshape(1, -1)

    gathered = row_total == 8 and joining_query.shape[0] % 16 == 0
    stacked = jnp.stack([joining_query, joining_key, joining_value], 0)
    if gathered:
        core = lax.rem(lax.axis_index("tok"), 2)
        column = width // 2
        piece = lax.dynamic_slice_in_dim(stacked, core * column, column, 2)[None]
        far = over_stage(piece, ORDER_JOIN, 0, "weights_first")

    x0 = tokens.reshape(here, width)
    x2 = over_bit(x0, 1, "row_far")
    x1 = over_bit(x0, 0, "row_near")
    seg = segments.reshape(batches, length)
    with jax.named_scope("segments"):
        segs = [seg] + [swap(seg, lambda d, flip=flip: d ^ flip) for flip in (1, 2, 3)]
    if gathered:
        far = mark(far)
    if gathered:
        near = mark(jnp.concatenate([piece, gate(far)], 0))
        far = over_stage(near, ORDER_JOIN, 1, "weights_second")
    bank = mark(
        jnp.concatenate([gate(query_weight), key_weight, value_weight, out_weight, adapter_down], 1)
    )
    x01 = mark(jnp.concatenate([x0, gate(x1)], 0))
    segs = mark(segs)
    x2 = mark(x2)
    x3 = over_bit(x2, 0, "row_cross")
    if gathered:
        far = mark(far)
        third = [over_stage(part, ORDER_JOIN, 2, "weights_third") for part in (near, far)]
    else:
        jw = (lax.all_gather(stacked, "rows", axis=1, tiled=True),)

    x3 = mark(x3)
    qs, keys, values, probs, attended, n1, rs1 = call(
        attend_kernel,
        "attend",
        6,
        (
            shape((here, width)), shape((4 * here, width)), shape((4 * here, width)),
            shape((batches * pairs, 4 * length, 2 * length)), shape((here, width)),
            shape((here, width), F32), shape((here, 128), F32),
        ),
        (VM,) * 7,
        (VM,) * 10,
        [pltpu.VMEM((4 * length, length), F32)],
        x01, x2, x3, *segs, bank,
        gate(row(attend_gain)), row(attend_bias),
    )
    if gathered:
        n1 = mark(n1)
        third = mark(third)
        jw = (near, far, *third)
        jw += tuple(over_bit(gate(part), 0, "weights_core") for part in jw)
    active, slope_z, n2, rs2, bottle, slope_t = call(
        feed_kernel,
        "feed",
        3,
        (
            shape((here, hidden_units)), shape((here, hidden_units)), shape((here, width), F32),
            shape((here, 128), F32), shape((here, width)), shape((here, width)),
        ),
        (VM,) * 6,
        (VM,) * 9,
        [],
        n1, row(attend_gain), row(attend_bias), inner_weight, row(inner_bias), outer_weight,
        gate(row(middle_gain)), row(middle_bias), bank,
    )
    n2 = mark(n2)

    waiting = []

    def later(values, travel, put):
        waiting.append((values, travel, put, len(waiting)))

    def start_waiting():
        for values, travel, put, place in waiting:
            put(travel(values if place == len(waiting) - 1 else gate(values)))
        waiting.clear()

    class Stream:
        def __init__(self, name, orders, rows_each):
            self.name, self.orders, self.rows_each, self.count = name, orders, rows_each, 0

        def send(self, values, stage, label, into="got"):
            def travel(operand):
                with jax.named_scope(f"{self.name}_{label}"):
                    if stage is None:
                        return over_bit(operand, 0)
                    return over_stage(operand, self.orders, stage)

            later(values, travel, lambda result: setattr(self, into, result))

        def begin(self, keep, send):
            self.keep, self.rows = keep, HALF * self.rows_each
            self.send(mark(send), None, "core")

        def step(self):
            stage, self.count = self.count, self.count + 1
            label = f"step_{stage}"
            keep, got = self.keep, gate(self.got)
            if stage < 4:
                middle = self.rows // 2
                send = mark(keep[middle:] + got[middle:])
                self.send(send, stage, label)
                self.keep = jnp.concatenate(
                    [keep[:middle] + got[:middle], keep[self.rows :] + got[self.rows :]], 0
                )
                self.rows = middle
            elif stage == 4:
                block = keep + got
                for bit in range(5, devices.bit_length() - 1):
                    block = block + over_bit(block, bit)
                self.extra = block[self.rows_each :]
                self.keep = mark(block[: self.rows_each])
                self.send(self.keep, 3, label)
            elif stage < 8:
                self.keep = mark(jnp.concatenate([keep, got], 0))
                self.send(self.keep, 7 - stage, label)
                if stage == 7:
                    self.send(self.keep, None, "sibling", "sibling")
            else:
                self.got, self.sibling = mark((got, self.sibling))
                self.send(self.got, None, "upper", "upper")

        def parts(self):
            return self.keep, self.got, self.sibling, getattr(self, "upper", None)

    def finish(stream, outs, layout, name, vector=None, whose=(0, 1), kept=()):
        sources = stream.parts()[2 * whose[0] : 2 * whose[-1] + 2]
        sources = list(sources[:-1]) + [gate(sources[-1])]
        vectors = [] if vector is None else [vector]
        small = [] if vector is None else [shape((1, width), F32)] * 6 + [shape((1, hidden_units), F32)]
        rows = sources[0].shape[0] * 2 * len(whose)
        first = len(sources) + len(vectors)
        out = call(
            functools.partial(
                finish_kernel, stream.orders, layout, whose, vector is not None, len(sources), len(kept)
            ),
            name,
            2,
            tuple(outs) + tuple(small),
            (ANY,) * len(outs) + (VM,) * len(small),
            (VM,) * first + (ANY,) * len(kept),
            [pltpu.VMEM((rows, width), F32), pltpu.SemaphoreType.DMA((8,))],
            *sources, *vectors, *kept,
            aliases=[(first + index, index) for index in range(len(kept))],
        )
        out = list(out)
        out[0] = mark(out[0])
        return out

    blocks = hidden_units // width
    square = shape((width, width), F32)
    each = lambda count: count * width // GROUP
    streams = {
        "J": Stream("joining_sum", ORDERS["J"], each(3)),
        "U": Stream("outer_sum", ORDERS["U"], each(blocks)),
        "I": Stream("inner_sum", ORDERS["I"], each(blocks + 1)),
        "T": Stream("attend_sum", ORDERS["T"], each(3)),
    }
    done = {}

    half_rows = lambda count: count * width // 2
    up = adapter_up.reshape(adapters * bottleneck, width)

    def joining_step():
        done["output"], keep, send, done["dhp"], done["dt"], done["vec_final"] = call(
            functools.partial(joining_kernel, gathered, bottleneck, adapters),
            "joining",
            8,
            (
                shape((here, width)), shape((half_rows(3), width)), shape((half_rows(3), width)),
                shape((here, width), F32), shape((here, width)), shape((8, width), F32),
            ),
            (VM,) * 6,
            (VM,) * (9 + len(jw)),
            [
                pltpu.VMEM((3, width, width), BF), pltpu.VMEM((3, here, width), BF),
                pltpu.VMEM((3, here, width), BF),
            ],
            n2, row(middle_gain), row(middle_bias), bottle, slope_t, up, cotangent.reshape(here, width),
            row(final_gain), row(final_bias), *jw,
        )
        streams["J"].begin(keep, send)

    def outer_step():
        done["d2"], done["vec_middle"], keep, send = call(
            outer_back_kernel,
            "outer_back",
            4,
            (
                shape((here, width), F32), shape((8, width), F32),
                shape((half_rows(blocks), width)), shape((half_rows(blocks), width)),
            ),
            (VM,) * 4,
            (VM,) * 7,
            [],
            done["dhp"], done["dt"], bank, n2, rs2, gate(row(middle_gain)), active,
        )
        streams["U"].begin(keep, send)

    def inner_step():
        done["d1"], done["vec"], keep, send = call(
            inner_back_kernel,
            "inner_back",
            6,
            (
                shape((here, width), F32), shape((16, width)),
                shape((half_rows(blocks + 1), width)), shape((half_rows(blocks + 1), width)),
            ),
            (VM,) * 4,
            (VM,) * 11,
            [pltpu.VMEM((here, hidden_units), BF), pltpu.VMEM((here, width), BF)],
            done["d2"], slope_z, inner_weight, outer_weight, n1, rs1, gate(row(attend_gain)),
            row(attend_bias), attended, done["vec_final"], done["vec_middle"],
        )
        streams["I"].begin(keep, send)

    def attend_step():
        keep, send, done["dq"], done["dk"], done["dv"] = call(
            attend_back_kernel,
            "attend_back",
            8,
            (
                shape((half_rows(3) + 16, width)), shape((half_rows(3) + 16, width)),
                shape((here, width)), shape((4 * here, width)), shape((4 * here, width)),
            ),
            (VM,) * 5,
            (VM,) * 11,
            [pltpu.VMEM((here, width), BF), pltpu.VMEM((4 * here, width), BF)],
            done["d1"], bank, attended, qs, keys, values, probs, x01, x2, x3, gate(done["vec"]),
        )
        streams["T"].begin(keep, send)

    def input_step():
        own, keep, send = call(
            input_back_kernel,
            "input_back",
            2,
            (shape((here, width), F32), shape((here, width)), shape((2 * here, width))),
            (VM,) * 3,
            (VM,) * 5,
            [],
            gate(done["d1"]), done["dq"], done["dk"], done["dv"], bank,
        )
        keep = mark(keep)
        done["gi"] = (own, keep)
        later(send, lambda values: over_bit(values, 0), lambda result: done.update(near=result))

    kernels = {"KJ": joining_step, "KU": outer_step, "KI": inner_step, "KT": attend_step, "KG": input_step}

    def run(plan):
        for step in [step for group in plan for step in group + (None,)]:
            if step is None:
                start_waiting()
            elif step in kernels:
                kernels[step]()
            elif step == "fJ":
                done["J"] = finish(streams["J"], [square] * 3, THREE, "finish_joining")
            elif step == "fU":
                done["U"] = finish(
                    streams["U"], [shape((hidden_units, width), F32)], ((0, 1, False),), "finish_outer"
                )
            elif step == "fI":
                done["I"] = finish(
                    streams["I"], [shape((width, hidden_units), F32), square],
                    ((0, blocks // 2, True), (1, 1, False)), "finish_inner",
                )
            elif step == "fT":
                done["T"] = finish(
                    streams["T"], [square] * 3, THREE, "finish_attend", streams["T"].extra, (1,), done["hT"]
                )
            elif step == "hT":
                done["hT"] = finish(streams["T"], [square] * 3, THREE, "finish_half", whose=(0,))
            elif step == "g0":
                got = gate(done["near"])
                send = mark(done["gi"][1] + got[here:])
                later(send, lambda values: over_bit(values, 1), lambda result: done.update(far=result))
                done["near"] = got[:here]
            elif step == "g1":
                far = gate(done["far"])
                done["input"] = mark(low(done["gi"][0] + done["near"].astype(F32) + far.astype(F32)))
            else:
                streams[step].step()

    run(PLAN)
    last, inner, out_grad = done["T"], done["I"][0], done["I"][1]
    outer, joining, output, input_grad = done["U"][0], done["J"], done["output"], done["input"]
    flat = lambda values: values.reshape(-1)
    return (
        output.reshape(tokens.shape), input_grad.reshape(tokens.shape),
        last[0], last[1], last[2], out_grad, flat(last[3]), flat(last[4]),
        inner, flat(last[9]), outer, flat(last[5]), flat(last[6]),
        joining[0], joining[1], joining[2], flat(last[7]), flat(last[8]),
    )


def solution(mesh):
    return jax.shard_map(
        functools.partial(per_device, mesh.shape["rows"]),
        mesh=mesh,
        in_specs=(
            P(None, "rows", "tok", None), P(None, "rows", "tok"), P(None, "rows", "tok", None),
        ) + (P(),) * 13 + (P("rows", None),) * 3 + (P(),) * 2,
        out_specs=(P(None, "rows", "tok", None),) * 2 + (P(),) * 16,
        check_vma=False,
    )
```

```python
import functools

import jax
import jax.numpy as jnp
from jax import lax
from jax.experimental import pallas as pl
from jax.experimental.pallas import tpu as pltpu
from jax.sharding import PartitionSpec as P

HEAD = 64
AXES = ("rows", "tok")
BF = jnp.bfloat16
F32 = jnp.float32
norm_eps = 1e-06

ORDER_XY = ((1, 2, 3, 4), (2, 1, 3, 4))
ORDER_YX = ((2, 1, 3, 4), (1, 2, 3, 4))
ORDER_Z = ((3, 4, 1, 2), (4, 3, 2, 1))
ORDER_ZY = ((4, 3, 1, 2), (3, 4, 2, 1))
ORDERS = {"J": ORDER_XY, "U": ORDER_Z, "I": ORDER_XY, "T": ORDER_XY}
ORDER_JOIN = ((2, 4, 3), (4, 3, 2))
GROUP = 32
THREE = ((0, 1, False), (1, 1, False), (2, 1, False))
PLAN = (
    ("KJ",), ("KU",), ("KI",), ("J", "U",), ("I",), ("KT",), ("KG", "J", "U", "I", "T",), ("I", "U",),
    ("T",), ("I", "J", "g0", "U", "T",), ("I",), ("J", "U",), ("I",), ("U", "T", "J",), ("J",),
    ("I", "U", "T",), ("g1",), ("J",), ("T",), ("I", "J", "U",), ("I", "T",), ("J", "T",), ("U",),
    ("fI", "fU",), ("fJ", "T",), ("hT",), ("fT",),
)
HALF = GROUP // 2

VM = pl.BlockSpec(memory_space=pltpu.VMEM)
ANY = pl.BlockSpec(memory_space=pl.ANY)


def dot(left, right):
    return jnp.dot(left, right, preferred_element_type=F32)


def dot_tn(left, right):
    return lax.dot_general(left, right, (((0,), (0,)), ((), ())), preferred_element_type=F32)


def dot_nt(left, right):
    return lax.dot_general(left, right, (((1,), (1,)), ((), ())), preferred_element_type=F32)


def low(values):
    return values.astype(BF)


def normalize(values, gain, shift):
    centered = values - jnp.mean(values, -1, keepdims=True)
    inv_std = lax.rsqrt(jnp.mean(centered * centered, -1, keepdims=True) + norm_eps)
    unit = centered * inv_std
    return unit * gain + shift, unit, inv_std


def normalize_back(upstream, unit, inv_std, gain):
    grad_unit = upstream * gain
    projected = grad_unit - jnp.mean(grad_unit, -1, keepdims=True)
    projected = projected - unit * jnp.mean(grad_unit * unit, -1, keepdims=True)
    gain_term = jnp.sum(upstream * unit, 0, keepdims=True)
    return projected * inv_std, gain_term, jnp.sum(upstream, 0, keepdims=True)


def gelu_both(values):
    normal_cdf = 0.5 * (1.0 + lax.erf(values * 0.7071067811865476))
    slope = normal_cdf + values * jnp.exp(-0.5 * values * values) * 0.3989422804014327
    return values * normal_cdf, slope


def device_number():
    return lax.axis_index("rows") * 4 + lax.axis_index("tok")


def bit_of(number, bit):
    return lax.rem(lax.div(number, 1 << bit), 2)


def own_place(number, orders, core):
    def along(order):
        total = 0
        for bit in order:
            total = total * 2 + bit_of(number, bit)
        return total

    return jnp.where(core == 0, along(orders[0]), along(orders[1]))


def put_blocks(target, values, first_row, place, rows_each):
    row = first_row
    while row < first_row + values.shape[0]:
        block, within = divmod(row, rows_each)
        count = min(rows_each - within, first_row + values.shape[0] - row)
        spot = jnp.bitwise_xor(place, block) * rows_each + within
        target[pl.ds(pl.multiple_of(spot, 16), count), :] = values[row - first_row : row - first_row + count, :]
        row += count


def halves(keep, send, orders):
    me = device_number()
    core = bit_of(me, 0)
    return (
        (keep, core, own_place(me, orders, core)),
        (send, 1 - core, own_place(me, orders, 1 - core)),
    )


def half_columns(ref, half, begin=0, count=None):
    size = ref.shape[1] // 2
    count = size if count is None else count
    return ref[:, pl.ds(pl.multiple_of(half * size + begin, 128), count)]


def of_bank(bank, index):
    width = bank.shape[0]
    return bank[:, index * width : (index + 1) * width]


def row_slices(ref, batch, length, lanes):
    here = ref.shape[0] // 4
    begins = [place * here + batch * length for place in range(4)]
    return jnp.concatenate([ref[begin : begin + length, lanes] for begin in begins], 0)


def attend_kernel(
    x01, x2, x3, seg0, seg1, seg2, seg3, bank, ag, ab,
    qs_ref, k_ref, v_ref, p_ref, o_ref, n1_ref, rs1_ref, bias,
):
    tokens_here, width = x2.shape
    batches = seg0.shape[0]
    length = tokens_here // batches
    qs_ref[...] = low(low(dot(x01[:tokens_here, :], of_bank(bank, 0))) * HEAD ** (-0.5))
    row = 0
    for piece in (x01, x2, x3):
        span = slice(row, row + piece.shape[0])
        k_ref[span, :] = low(dot(piece[...], of_bank(bank, 1)))
        v_ref[span, :] = low(dot(piece[...], of_bank(bank, 2)))
        row += piece.shape[0]
    segments = [ref[...].astype(F32) for ref in (seg0, seg1, seg2, seg3)]
    lane = lax.broadcasted_iota(jnp.int32, (1, 2 * HEAD), 1)
    first = (lane < HEAD).astype(BF)
    second = (lane >= HEAD).astype(BF)
    for batch in range(batches):
        query_seg = segments[0][batch : batch + 1, :]
        for index, segment in enumerate(segments):
            row = segment[batch : batch + 1, :]
            key_seg = jnp.transpose(jnp.broadcast_to(row, (length, length)))
            bias[pl.ds(index * length, length), :] = jnp.where(key_seg == query_seg, 0.0, -1e30)
        both = jnp.concatenate([bias[...], bias[...]], 1)
        for pair in range(width // (2 * HEAD)):
            lanes = slice(pair * 2 * HEAD, (pair + 1) * 2 * HEAD)
            kp = row_slices(k_ref, batch, length, lanes)
            vp = row_slices(v_ref, batch, length, lanes)
            qp = qs_ref[batch * length : (batch + 1) * length, lanes]
            stacked = jnp.concatenate([qp * first, qp * second], 0)
            scores = dot_nt(kp, stacked) + both
            exps = jnp.exp(scores - jnp.max(scores, 0, keepdims=True))
            probs = low(exps * (1.0 / jnp.sum(exps, 0, keepdims=True)))
            p_ref[batch * (width // (2 * HEAD)) + pair] = probs
            mixed = dot_tn(vp, probs)
            joined = jnp.concatenate([mixed[:HEAD, :length], mixed[HEAD:, length:]], 0)
            o_ref[batch * length : (batch + 1) * length, lanes] = low(jnp.transpose(joined))
    residual = x01[:tokens_here, :].astype(F32) + dot(o_ref[...], of_bank(bank, 3))
    _, unit, inv_std = normalize(residual, ag[...], ab[...])
    n1_ref[...] = unit
    rs1_ref[...] = jnp.broadcast_to(inv_std, rs1_ref.shape)


def feed_kernel(
    n1_ref, ag, ab, wi, bi, wu, mg, mb, bank, u_ref, sz_ref, n2_ref, rs2_ref, c_ref, st_ref
):
    width = n1_ref.shape[1]
    outer = n1_ref[...] * ag[...] + ab[...]
    al = low(outer)
    for part in range(wi.shape[1] // width):
        span = slice(part * width, (part + 1) * width)
        inner = dot(al, wi[:, span]) + bi[:, span]
        active, slope = gelu_both(inner)
        u_ref[:, span] = low(active)
        sz_ref[:, span] = low(slope)
        outer = outer + dot(low(active), wu[span, :])
    hidden, unit, inv_std = normalize(outer, mg[...], mb[...])
    n2_ref[...] = unit
    rs2_ref[...] = jnp.broadcast_to(inv_std, rs2_ref.shape)
    active, slope = gelu_both(dot(low(hidden), of_bank(bank, 4)))
    c_ref[...] = low(active)
    st_ref[...] = low(slope)


def joining_kernel(
    gathered, bottleneck, adapters, n2_ref, mg, mb, c_ref, st_ref, up, cot, fg, fb, *rest
):
    if gathered:
        jw_in, rest = rest[:8], rest[8:]
    else:
        jw_in, rest = rest[:1], rest[1:]
    out_ref, keep, send, dhp_ref, dt_ref, vec_ref, wj, left, right = rest
    width = n2_ref.shape[1]
    scale = width ** (-0.5)
    me = device_number()
    core = bit_of(me, 0)
    if gathered:
        shard, column = jw_in[0].shape[2:]
        for which in range(2):
            half = core if which == 0 else 1 - core
            columns = pl.ds(pl.multiple_of(half * column, column), column)
            for spot in range(8):
                flips = [sum(((spot >> i) & 1) << (order[i] - 2) for i in range(3)) for order in ORDER_JOIN]
                owner = jnp.bitwise_xor(lax.div(me, 4), jnp.where(half == 0, flips[0], flips[1]))
                rows = pl.ds(pl.multiple_of(owner * shard, shard), shard)
                for matrix in range(3):
                    wj[matrix, rows, columns] = jw_in[which * 4 + spot // 2][spot % 2, matrix]
    else:
        wj[...] = jw_in[0][...]
    hidden = n2_ref[...] * mg[...] + mb[...]
    hidden_low = low(hidden)
    cf = c_ref[...].astype(F32)
    row_group = lax.broadcasted_iota(jnp.int32, (width, 128), 0) // bottleneck
    column_of = lax.broadcasted_iota(jnp.int32, (width, 128), 1)
    member = (row_group == column_of).astype(BF)
    valid = lax.broadcasted_iota(jnp.int32, (1, 128), 1) < adapters

    def per_adapter(values):
        high = low(values)
        rest_of = low(values - high.astype(F32))
        return dot(high, member) + dot(rest_of, member)

    fq = low(dot(hidden_low, wj[0]))
    probe = low(dot_nt(fq, wj[1]))
    probe_f = probe.astype(F32)
    up_probe = dot_nt(probe, up[...])
    scores = (
        per_adapter(cf * up_probe) + jnp.sum(hidden * probe_f, -1, keepdims=True)
    ) * scale
    scores = jnp.where(valid, scores, -1e30)
    exps = jnp.exp(scores - jnp.max(scores, -1, keepdims=True))
    weights = exps * (1.0 / jnp.sum(exps, -1, keepdims=True))
    weights_low = low(weights)
    weights_wide = dot_nt(weights_low, member)
    weights_sum = jnp.sum(weights_low.astype(F32), -1, keepdims=True)
    mixed = low(weights_sum * hidden + dot(low(weights_wide * cf), up[...]))
    final, unit, inv_std = normalize(hidden + dot(mixed, wj[2]), fg[...], fb[...])
    out_ref[...] = low(final)
    d3, gain_term, shift_term = normalize_back(cot[...].astype(F32), unit, inv_std, fg[...])
    vec_ref[...] = jnp.concatenate(
        [gain_term, shift_term, jnp.zeros((vec_ref.shape[0] - 2, width), F32)], 0
    )
    dfo = low(d3)
    left[2] = mixed
    right[2] = dfo
    dm = low(dot_nt(dfo, wj[2]))
    dm_f = dm.astype(F32)
    up_dm = dot_nt(dm, up[...])
    dw = per_adapter(cf * up_dm) + jnp.sum(hidden * dm_f, -1, keepdims=True)
    df = low(weights * (dw - jnp.sum(weights * dw, -1, keepdims=True)))
    df_wide = dot_nt(df, member)
    df_sum = jnp.sum(df.astype(F32), -1, keepdims=True)
    dr = low((df_sum * hidden + dot(low(df_wide * cf), up[...])) * scale)
    left[1] = dr
    right[1] = fq
    dfq = low(dot(dr, wj[1]))
    left[0] = hidden_low
    right[0] = dfq
    for target, half, place in halves(keep, send, ORDERS["J"]):
        for matrix in range(3):
            term = low(dot_tn(half_columns(left.at[matrix], half), right[matrix]))
            put_blocks(target, term, matrix * (width // 2), place, 3 * width // GROUP)
    dc = weights_wide * up_dm + (df_wide * scale) * up_probe
    dt_ref[...] = low(dc * st_ref[...].astype(F32))
    dhp_ref[...] = (
        d3 + weights_sum * dm_f + (df_sum * scale) * probe_f + dot_nt(dfq, wj[0])
    )


def outer_back_kernel(
    dhp_ref, dt_ref, bank, n2_ref, rs2_ref, mg, u_ref, d2_ref, vec_ref, keep, send
):
    width = dhp_ref.shape[1]
    hidden_grad = dhp_ref[...] + dot_nt(dt_ref[...], of_bank(bank, 4))
    d2, mg_term, mb_term = normalize_back(hidden_grad, n2_ref[...], rs2_ref[:, :1], mg[...])
    d2_ref[...] = d2
    dfw = low(d2)
    units = u_ref.shape[1]
    for target, half, place in halves(keep, send, ORDERS["U"]):
        for begin in range(0, units // 2, width):
            term = low(dot_tn(half_columns(u_ref, half, begin, width), dfw))
            put_blocks(target, term, begin, place, units // GROUP)
    vec_ref[...] = jnp.concatenate([mg_term, mb_term, jnp.zeros((vec_ref.shape[0] - 2, width), F32)], 0)


def inner_back_kernel(
    d2_ref, sz_ref, wi, wu, n1_ref, rs1_ref, ag, ab, o_ref, vec_final, vec_middle,
    d1_ref, vec_ref, keep, send, dz_scr, dao_scr,
):
    width = d2_ref.shape[1]
    total = d2_ref[...]
    dfw = low(total)
    al = low(n1_ref[...] * ag[...] + ab[...])
    bias_terms = []
    parts = wi.shape[1] // width
    for part in range(parts):
        span = slice(part * width, (part + 1) * width)
        dz = low(dot_nt(dfw, wu[span, :]) * sz_ref[:, span].astype(F32))
        bias_terms.append(jnp.sum(dz.astype(F32), 0, keepdims=True))
        dz_scr[:, span] = dz
        total = total + dot_nt(dz, wi[:, span])
    d1, ag_term, ab_term = normalize_back(total, n1_ref[...], rs1_ref[:, :1], ag[...])
    d1_ref[...] = d1
    dao_scr[...] = low(d1)
    units = wi.shape[1]
    rows_each = (units + width) // GROUP
    for target, half, place in halves(keep, send, ORDERS["I"]):
        for begin in range(0, units // 2, width):
            term = low(dot_tn(al, half_columns(dz_scr, half, begin, width)))
            put_blocks(target, term, begin, place, rows_each)
        term = low(dot_tn(half_columns(o_ref, half), dao_scr[...]))
        put_blocks(target, term, units // 2, place, rows_each)
    rows = [ag_term, ab_term, vec_middle[0:1, :], vec_middle[1:2, :], vec_final[0:1, :], vec_final[1:2, :]]
    rows += bias_terms
    rows.append(jnp.zeros((vec_ref.shape[0] - len(rows), width), F32))
    vec_ref[...] = low(jnp.concatenate(rows, 0))


def attend_back_kernel(
    d1_ref, bank, o_ref, qs_ref, k_ref, v_ref, p_ref, x01, x2, x3, vec_ref,
    keep, send, dq_ref, dk_ref, dv_ref, do_scr, row_x,
):
    tokens_here, width = x2.shape
    length = p_ref.shape[2] // 2
    batches = tokens_here // length
    pairs = width // (2 * HEAD)
    do_scr[...] = low(dot_nt(low(d1_ref[...]), of_bank(bank, 3)))
    lane = lax.broadcasted_iota(jnp.int32, (1, 2 * HEAD), 1)
    first = (lane < HEAD).astype(BF)
    second = (lane >= HEAD).astype(BF)
    for batch in range(batches):
        here = slice(batch * length, (batch + 1) * length)
        spans = [
            slice(index * tokens_here + batch * length, index * tokens_here + (batch + 1) * length)
            for index in range(4)
        ]
        for pair in range(pairs):
            lanes = slice(pair * 2 * HEAD, (pair + 1) * 2 * HEAD)
            kp = row_slices(k_ref, batch, length, lanes)
            vp = row_slices(v_ref, batch, length, lanes)
            qp = qs_ref[here, lanes]
            dop = do_scr[here, lanes]
            q_stacked = jnp.concatenate([qp * first, qp * second], 0)
            do_stacked = jnp.concatenate([dop * first, dop * second], 0)
            probs = p_ref[batch * pairs + pair]
            op = o_ref[here, lanes].astype(F32)
            product = dop.astype(F32) * op
            high = low(product)
            rest = low(product - high.astype(F32))
            spread = jnp.concatenate([high * first, high * second], 0)
            spread_rest = jnp.concatenate([rest * first, rest * second], 0)
            ones = jnp.ones((8, 2 * HEAD), BF)
            shift = (dot_nt(ones, spread) + dot_nt(ones, spread_rest))[:1, :]
            ds = low(probs.astype(F32) * (dot_nt(vp, do_stacked) - shift))
            dv = low(dot(probs, do_stacked))
            dk = low(dot(ds, q_stacked))
            for index, span in enumerate(spans):
                rows = slice(index * length, (index + 1) * length)
                dk_ref[span, lanes] = dk[rows, :]
                dv_ref[span, lanes] = dv[rows, :]
            mixed = dot_tn(kp, ds)
            joined = jnp.concatenate([mixed[:HEAD, :length], mixed[HEAD:, length:]], 0)
            dq_ref[here, lanes] = low(jnp.transpose(joined) * HEAD ** (-0.5))
    row_x[: 2 * tokens_here, :] = x01[...]
    row_x[2 * tokens_here : 3 * tokens_here, :] = x2[...]
    row_x[3 * tokens_here :, :] = x3[...]
    rows_each = 3 * width // GROUP
    for target, half, place in halves(keep, send, ORDERS["T"]):
        terms = (
            dot_tn(half_columns(x01.at[:tokens_here, :], half), dq_ref[...]),
            dot_tn(half_columns(row_x, half), dk_ref[...]),
            dot_tn(half_columns(row_x, half), dv_ref[...]),
        )
        for matrix, term in enumerate(terms):
            put_blocks(target, low(term), matrix * (width // 2), place, rows_each)
        target[HALF * rows_each :, :] = vec_ref[...]


def input_back_kernel(d1_ref, dq_ref, dk_ref, dv_ref, bank, gi_own, gi_keep, gi_send):
    tokens_here = d1_ref.shape[0]
    parts = []
    for index in range(4):
        span = slice(index * tokens_here, (index + 1) * tokens_here)
        parts.append(dot_nt(dk_ref[span, :], of_bank(bank, 1)) + dot_nt(dv_ref[span, :], of_bank(bank, 2)))
    gi_own[...] = parts[0] + d1_ref[...] + dot_nt(dq_ref[...], of_bank(bank, 0))
    gi_keep[...] = low(parts[2])
    gi_send[:tokens_here, :] = low(parts[1])
    gi_send[tokens_here:, :] = low(parts[3])


def finish_kernel(orders, layout, whose, with_vec, parts, kept, *rest):
    sources, rest = rest[:parts], rest[parts:]
    if with_vec:
        vec, rest = rest[0], rest[1:]
    rest = rest[kept:]
    full, sems = rest[-2:]
    outs = rest[:-2]
    me = device_number()
    core = bit_of(me, 0)
    each = sources[0].shape[0] // (HALF // 2)
    half_rows = HALF * each
    width = full.shape[1]
    copies = []
    for number, which in enumerate(whose):
        lower, upper = sources[2 * number : 2 * number + 2]
        half = core if which == 0 else 1 - core
        place = own_place(me, orders, half)
        base = number * half_rows
        for spot in range(HALF):
            source = lower if spot < HALF // 2 else upper
            begin = (spot % (HALF // 2)) * each
            block = jnp.bitwise_xor(place, spot)
            full[pl.ds(pl.multiple_of(base + block * each, 8), each), :] = source[
                begin : begin + each, :
            ].astype(F32)
        row = base
        for out, pieces, by_column in layout:
            for piece in range(pieces):
                target = outs[out]
                if by_column:
                    size = target.shape[0]
                    column = pl.multiple_of((half * pieces + piece) * width, width)
                    target = target.at[:, pl.ds(column, width)]
                else:
                    size = target.shape[0] // 2
                    target = target.at[pl.ds(pl.multiple_of(half * size, size), size), :]
                source = full.at[pl.ds(row, size), :]
                copies.append(pltpu.make_async_copy(source, target, sems.at[len(copies)]))
                copies[-1].start()
                row += size
    if with_vec:
        values = vec[...].astype(F32)
        small = [out for out in outs if out.shape[0] == 1]
        for index in range(6):
            small[index][...] = values[index : index + 1, :]
        for part in range(small[6].shape[1] // width):
            small[6][:, part * width : (part + 1) * width] = values[6 + part : 7 + part, :]
    for copy in copies:
        copy.wait()


def call(kernel, name, microseconds, out_shapes, out_specs, in_specs, scratch, *operands, aliases=()):
    return pl.pallas_call(
        kernel,
        out_shape=out_shapes,
        in_specs=in_specs,
        out_specs=out_specs,
        scratch_shapes=scratch,
        input_output_aliases=dict(aliases),
        compiler_params=pltpu.CompilerParams(vmem_limit_bytes=32 * 1024 * 1024),
        cost_estimate=pl.CostEstimate(
            flops=int(microseconds * 1e4), bytes_accessed=int(microseconds * 1e2), transcendentals=0
        ),
        name=name,
    )(*operands)


def shape(dims, kind=BF):
    return jax.ShapeDtypeStruct(dims, kind)


def per_device(
    row_total,
    tokens, segments, cotangent, query_weight, key_weight, value_weight, out_weight,
    attend_gain, attend_bias, inner_weight, inner_bias, outer_weight, middle_gain, middle_bias,
    adapter_down, adapter_up, joining_query, joining_key, joining_value, final_gain, final_bias,
):
    batches, row_count, length, width = tokens.shape
    here = batches * row_count * length
    hidden_units = inner_weight.shape[1]
    adapters, bottleneck = adapter_up.shape[0], adapter_up.shape[1]
    devices = row_total * 4
    pairs = width // (2 * HEAD)

    def swap(values, partner):
        return lax.ppermute(values, AXES, [(d, partner(d)) for d in range(devices)])

    def over_bit(values, bit, label="over_bit"):
        with jax.named_scope(label):
            return swap(values, lambda d: d ^ (1 << bit))

    def over_stage(values, orders, stage, label="over_stage"):
        with jax.named_scope(label):
            return swap(values, lambda d: d ^ (1 << orders[d & 1][stage]))

    token = [lax.create_token()]

    def gate(values):
        return lax.optimization_barrier((token[0], values))[1]

    def mark(values):
        token[0], values = lax.optimization_barrier((token[0], values))
        return values

    row = lambda vector: vector.reshape(1, -1)

    gathered = row_total == 8 and joining_query.shape[0] % 16 == 0
    stacked = jnp.stack([joining_query, joining_key, joining_value], 0)
    if gathered:
        core = lax.rem(lax.axis_index("tok"), 2)
        column = width // 2
        piece = lax.dynamic_slice_in_dim(stacked, core * column, column, 2)[None]
        far = over_stage(piece, ORDER_JOIN, 0, "weights_first")

    x0 = tokens.reshape(here, width)
    x2 = over_bit(x0, 1, "row_far")
    x1 = over_bit(x0, 0, "row_near")
    seg = segments.reshape(batches, length)
    with jax.named_scope("segments"):
        segs = [seg] + [swap(seg, lambda d, flip=flip: d ^ flip) for flip in (1, 2, 3)]
    if gathered:
        far = mark(far)
    if gathered:
        near = mark(jnp.concatenate([piece, gate(far)], 0))
        far = over_stage(near, ORDER_JOIN, 1, "weights_second")
    bank = mark(
        jnp.concatenate([gate(query_weight), key_weight, value_weight, out_weight, adapter_down], 1)
    )
    x01 = mark(jnp.concatenate([x0, gate(x1)], 0))
    segs = mark(segs)
    x2 = mark(x2)
    x3 = over_bit(x2, 0, "row_cross")
    if gathered:
        far = mark(far)
        third = [over_stage(part, ORDER_JOIN, 2, "weights_third") for part in (near, far)]
    else:
        jw = (lax.all_gather(stacked, "rows", axis=1, tiled=True),)

    x3 = mark(x3)
    qs, keys, values, probs, attended, n1, rs1 = call(
        attend_kernel,
        "attend",
        6,
        (
            shape((here, width)), shape((4 * here, width)), shape((4 * here, width)),
            shape((batches * pairs, 4 * length, 2 * length)), shape((here, width)),
            shape((here, width), F32), shape((here, 128), F32),
        ),
        (VM,) * 7,
        (VM,) * 10,
        [pltpu.VMEM((4 * length, length), F32)],
        x01, x2, x3, *segs, bank,
        gate(row(attend_gain)), row(attend_bias),
    )
    if gathered:
        n1 = mark(n1)
        third = mark(third)
        jw = (near, far, *third)
        jw += tuple(over_bit(gate(part), 0, "weights_core") for part in jw)
    active, slope_z, n2, rs2, bottle, slope_t = call(
        feed_kernel,
        "feed",
        3,
        (
            shape((here, hidden_units)), shape((here, hidden_units)), shape((here, width), F32),
            shape((here, 128), F32), shape((here, width)), shape((here, width)),
        ),
        (VM,) * 6,
        (VM,) * 9,
        [],
        n1, row(attend_gain), row(attend_bias), inner_weight, row(inner_bias), outer_weight,
        gate(row(middle_gain)), row(middle_bias), bank,
    )
    n2 = mark(n2)

    waiting = []

    def later(values, travel, put):
        waiting.append((values, travel, put, len(waiting)))

    def start_waiting():
        for values, travel, put, place in waiting:
            put(travel(values if place == len(waiting) - 1 else gate(values)))
        waiting.clear()

    class Stream:
        def __init__(self, name, orders, rows_each):
            self.name, self.orders, self.rows_each, self.count = name, orders, rows_each, 0

        def send(self, values, stage, label, into="got"):
            def travel(operand):
                with jax.named_scope(f"{self.name}_{label}"):
                    if stage is None:
                        return over_bit(operand, 0)
                    return over_stage(operand, self.orders, stage)

            later(values, travel, lambda result: setattr(self, into, result))

        def begin(self, keep, send):
            self.keep, self.rows = keep, HALF * self.rows_each
            self.send(mark(send), None, "core")

        def step(self):
            stage, self.count = self.count, self.count + 1
            label = f"step_{stage}"
            keep, got = self.keep, gate(self.got)
            if stage < 4:
                middle = self.rows // 2
                send = mark(keep[middle:] + got[middle:])
                self.send(send, stage, label)
                self.keep = jnp.concatenate(
                    [keep[:middle] + got[:middle], keep[self.rows :] + got[self.rows :]], 0
                )
                self.rows = middle
            elif stage == 4:
                block = keep + got
                for bit in range(5, devices.bit_length() - 1):
                    block = block + over_bit(block, bit)
                self.extra = block[self.rows_each :]
                self.keep = mark(block[: self.rows_each])
                self.send(self.keep, 3, label)
            elif stage < 8:
                self.keep = mark(jnp.concatenate([keep, got], 0))
                self.send(self.keep, 7 - stage, label)
                if stage == 7:
                    self.send(self.keep, None, "sibling", "sibling")
            else:
                self.got, self.sibling = mark((got, self.sibling))
                self.send(self.got, None, "upper", "upper")

        def parts(self):
            return self.keep, self.got, self.sibling, getattr(self, "upper", None)

    def finish(stream, outs, layout, name, vector=None, whose=(0, 1), kept=()):
        sources = stream.parts()[2 * whose[0] : 2 * whose[-1] + 2]
        sources = list(sources[:-1]) + [gate(sources[-1])]
        vectors = [] if vector is None else [vector]
        small = [] if vector is None else [shape((1, width), F32)] * 6 + [shape((1, hidden_units), F32)]
        rows = sources[0].shape[0] * 2 * len(whose)
        first = len(sources) + len(vectors)
        out = call(
            functools.partial(
                finish_kernel, stream.orders, layout, whose, vector is not None, len(sources), len(kept)
            ),
            name,
            2,
            tuple(outs) + tuple(small),
            (ANY,) * len(outs) + (VM,) * len(small),
            (VM,) * first + (ANY,) * len(kept),
            [pltpu.VMEM((rows, width), F32), pltpu.SemaphoreType.DMA((8,))],
            *sources, *vectors, *kept,
            aliases=[(first + index, index) for index in range(len(kept))],
        )
        out = list(out)
        out[0] = mark(out[0])
        return out

    blocks = hidden_units // width
    square = shape((width, width), F32)
    each = lambda count: count * width // GROUP
    streams = {
        "J": Stream("joining_sum", ORDERS["J"], each(3)),
        "U": Stream("outer_sum", ORDERS["U"], each(blocks)),
        "I": Stream("inner_sum", ORDERS["I"], each(blocks + 1)),
        "T": Stream("attend_sum", ORDERS["T"], each(3)),
    }
    done = {}

    half_rows = lambda count: count * width // 2
    up = adapter_up.reshape(adapters * bottleneck, width)

    def joining_step():
        done["output"], keep, send, done["dhp"], done["dt"], done["vec_final"] = call(
            functools.partial(joining_kernel, gathered, bottleneck, adapters),
            "joining",
            8,
            (
                shape((here, width)), shape((half_rows(3), width)), shape((half_rows(3), width)),
                shape((here, width), F32), shape((here, width)), shape((8, width), F32),
            ),
            (VM,) * 6,
            (VM,) * (9 + len(jw)),
            [
                pltpu.VMEM((3, width, width), BF), pltpu.VMEM((3, here, width), BF),
                pltpu.VMEM((3, here, width), BF),
            ],
            n2, row(middle_gain), row(middle_bias), bottle, slope_t, up, cotangent.reshape(here, width),
            row(final_gain), row(final_bias), *jw,
        )
        streams["J"].begin(keep, send)

    def outer_step():
        done["d2"], done["vec_middle"], keep, send = call(
            outer_back_kernel,
            "outer_back",
            4,
            (
                shape((here, width), F32), shape((8, width), F32),
                shape((half_rows(blocks), width)), shape((half_rows(blocks), width)),
            ),
            (VM,) * 4,
            (VM,) * 7,
            [],
            done["dhp"], done["dt"], bank, n2, rs2, gate(row(middle_gain)), active,
        )
        streams["U"].begin(keep, send)

    def inner_step():
        done["d1"], done["vec"], keep, send = call(
            inner_back_kernel,
            "inner_back",
            6,
            (
                shape((here, width), F32), shape((16, width)),
                shape((half_rows(blocks + 1), width)), shape((half_rows(blocks + 1), width)),
            ),
            (VM,) * 4,
            (VM,) * 11,
            [pltpu.VMEM((here, hidden_units), BF), pltpu.VMEM((here, width), BF)],
            done["d2"], slope_z, inner_weight, outer_weight, n1, rs1, gate(row(attend_gain)),
            row(attend_bias), attended, done["vec_final"], done["vec_middle"],
        )
        streams["I"].begin(keep, send)

    def attend_step():
        keep, send, done["dq"], done["dk"], done["dv"] = call(
            attend_back_kernel,
            "attend_back",
            8,
            (
                shape((half_rows(3) + 16, width)), shape((half_rows(3) + 16, width)),
                shape((here, width)), shape((4 * here, width)), shape((4 * here, width)),
            ),
            (VM,) * 5,
            (VM,) * 11,
            [pltpu.VMEM((here, width), BF), pltpu.VMEM((4 * here, width), BF)],
            done["d1"], bank, attended, qs, keys, values, probs, x01, x2, x3, gate(done["vec"]),
        )
        streams["T"].begin(keep, send)

    def input_step():
        own, keep, send = call(
            input_back_kernel,
            "input_back",
            2,
            (shape((here, width), F32), shape((here, width)), shape((2 * here, width))),
            (VM,) * 3,
            (VM,) * 5,
            [],
            gate(done["d1"]), done["dq"], done["dk"], done["dv"], bank,
        )
        keep = mark(keep)
        done["gi"] = (own, keep)
        later(send, lambda values: over_bit(values, 0), lambda result: done.update(near=result))

    kernels = {"KJ": joining_step, "KU": outer_step, "KI": inner_step, "KT": attend_step, "KG": input_step}

    def run(plan):
        for step in [step for group in plan for step in group + (None,)]:
            if step is None:
                start_waiting()
            elif step in kernels:
                kernels[step]()
            elif step == "fJ":
                done["J"] = finish(streams["J"], [square] * 3, THREE, "finish_joining")
            elif step == "fU":
                done["U"] = finish(
                    streams["U"], [shape((hidden_units, width), F32)], ((0, 1, False),), "finish_outer"
                )
            elif step == "fI":
                done["I"] = finish(
                    streams["I"], [shape((width, hidden_units), F32), square],
                    ((0, blocks // 2, True), (1, 1, False)), "finish_inner",
                )
            elif step == "fT":
                done["T"] = finish(
                    streams["T"], [square] * 3, THREE, "finish_attend", streams["T"].extra, (1,), done["hT"]
                )
            elif step == "hT":
                done["hT"] = finish(streams["T"], [square] * 3, THREE, "finish_half", whose=(0,))
            elif step == "g0":
                got = gate(done["near"])
                send = mark(done["gi"][1] + got[here:])
                later(send, lambda values: over_bit(values, 1), lambda result: done.update(far=result))
                done["near"] = got[:here]
            elif step == "g1":
                far = gate(done["far"])
                done["input"] = mark(low(done["gi"][0] + done["near"].astype(F32) + far.astype(F32)))
            else:
                streams[step].step()

    run(PLAN)
    last, inner, out_grad = done["T"], done["I"][0], done["I"][1]
    outer, joining, output, input_grad = done["U"][0], done["J"], done["output"], done["input"]
    flat = lambda values: values.reshape(-1)
    return (
        output.reshape(tokens.shape), input_grad.reshape(tokens.shape),
        last[0], last[1], last[2], out_grad, flat(last[3]), flat(last[4]),
        inner, flat(last[9]), outer, flat(last[5]), flat(last[6]),
        joining[0], joining[1], joining[2], flat(last[7]), flat(last[8]),
    )


def solution(mesh):
    return jax.shard_map(
        functools.partial(per_device, mesh.shape["rows"]),
        mesh=mesh,
        in_specs=(
            P(None, "rows", "tok", None), P(None, "rows", "tok"), P(None, "rows", "tok", None),
        ) + (P(),) * 13 + (P("rows", None),) * 3 + (P(),) * 2,
        out_specs=(P(None, "rows", "tok", None),) * 2 + (P(),) * 16,
        check_vma=False,
    )
```
